512 devices in a mesh: stream: 32 (over z, x), cross: 16 (over y, core).
Axes of the slice: x: 4, y: 8, z: 8, core: 2. Of those that a mesh axis runs over, the one named last changes fastest.
Arguments:
- adjoint: float32 [5, 128, 16384], P(None, 'stream', 'cross'), may hold values from -6 to 6
- source: float32 [5, 128, 16384], P(None, 'stream', 'cross'), may hold values from -30 to 30
- shape_grad: float32 [5, 128, 16384], P(None, 'stream', 'cross'), may hold values from -6 to 6
- lower_band: float32 [2, 5, 128, 16384], P(None, None, 'stream', 'cross'), may hold values from -1.5 to 0.5
- upper_band: float32 [3, 5, 128, 16384], P(None, None, 'stream', 'cross'), may hold values from -6 to 2, as said below
- jacobian: float32 [5, 5], replicated, may hold values from -2.5 to 2.5
- left_vectors: float32 [5, 5], replicated, may hold values from -1 to 2
- right_vectors: float32 [5, 5], replicated, may hold values from -1 to 2
- ctrl_local: int32 [128, 16384], P('stream', 'cross'), may hold values from 0 to 16383
Outputs:
- adjoint_next: float32 [5, 128, 16384], P(None, 'stream', 'cross')
- sensitivity: float32 [524288], P(('stream', 'cross'))
The draws below stay inside these ranges and needn't reach their ends.
Inputs may be any that keep to these rules, and one draw needn't show every extreme that they name: upper_band[0] lies in 0.5 to 2.
All inputs are finite; a program needn't handle non-finite values.
Results may differ from the reference program's by a relative error of at most 0.00029.
Values sent between devices are 32-bit elements; how exact they have to be, the bound alone decides.
A program may use at most 64 MiB of HBM per device.

```python
import jax
import jax.numpy as jnp
from jax import lax

NF = 5
NI_DEV = 4
NCTRL = 524288
NI = 128
NJ = 16384
NCTRL_SLAB = 16384


def draw_source(key, part):
    position = (jnp.arange(NI, dtype=jnp.float32) + 0.5) / NI
    growth = jnp.exp(jnp.log(3.0) * position)[None, :, None]
    rough = jnp.clip(jax.random.normal(jax.random.fold_in(key, 1), (NF, NI, NJ), jnp.float32), -8.0, 8.0)
    return rough * growth


def slow_rates(key, low, high):
    return jax.random.uniform(key, (NF, NI, NJ), jnp.float32, low, high)


def draw_lower_band(key, part):
    slow = slow_rates(jax.random.fold_in(key, 11), 0.8, 0.99)
    fast = jax.random.uniform(jax.random.fold_in(key, 12), (NF, 1, NJ), jnp.float32, 0.1, 0.5)
    fast = jnp.broadcast_to(fast, (NF, NI, NJ))
    return jnp.stack([-(slow + fast), slow * fast])


def draw_upper_band(key, part):
    slow = slow_rates(jax.random.fold_in(key, 21), 0.8, 0.99)
    fast = jax.random.uniform(jax.random.fold_in(key, 22), (NF, 1, NJ), jnp.float32, 0.1, 0.5)
    fast = jnp.broadcast_to(fast, (NF, NI, NJ))
    diagonal = jnp.exp(jax.random.uniform(jax.random.fold_in(key, 23), (NF, NI, NJ), jnp.float32, jnp.log(0.5), jnp.log(2.0)))
    return jnp.stack([diagonal, -(slow + fast) * diagonal, slow * fast * diagonal])


def draw_left_vectors(key, part):
    noise = jnp.clip(jax.random.normal(jax.random.fold_in(key, 31), (NF, NF), jnp.float32), -3.0, 3.0)
    return jnp.eye(NF, dtype=jnp.float32) + 0.3 * noise


def draw_right_vectors(key, part):
    noise = jnp.clip(jax.random.normal(jax.random.fold_in(key, 41), (NF, NF), jnp.float32), -3.0, 3.0)
    return jnp.eye(NF, dtype=jnp.float32) + 0.3 * noise


def plant(drawn, own_key, least, high):
    index_at = [jax.random.randint(jax.random.fold_in(own_key, axis), (), 0, length) for axis, length in enumerate(drawn.shape)]
    widest = drawn.shape.index(max(drawn.shape))
    neighbour = index_at[:widest] + [(index_at[widest] + 1) % drawn.shape[widest]] + index_at[widest + 1:]
    return drawn.at[tuple(index_at)].set(least).at[tuple(neighbour)].set(high)


def steps_of(stream_key, extent, shards, least, high):
    level = 1.0
    for axis_at, shards_of in shards:
        steps = jax.random.uniform(jax.random.fold_in(jax.random.fold_in(stream_key, 6), axis_at), (shards_of,), jnp.float32, least / len(shards), high / len(shards))
        level = level * jnp.repeat(jnp.exp(steps), extent[axis_at] // shards_of).reshape((-1,) + (1,) * (len(extent) - 1 - axis_at))
    return level


def scatter_about(key, shape, scale, most, pieces=(), kind=jnp.bfloat16):
    array = jax.random.normal(key, shape, jnp.float32) * scale
    if len(pieces) > 0:
        array = steps_of(key, shape, pieces, -0.22, 0.18) * array
    return jnp.clip(array, min=-most, max=most).astype(kind)


def setup_inputs(seed: int = 0) -> dict:
    key_of = jax.random.split(jax.random.key(seed), 10)
    adjoint = scatter_about(key_of[0], (NF, NI, NJ), 1.0, 6.0, ((1, 32), (2, 16)), jnp.float32)
    source = draw_source(jax.random.fold_in(key_of[9], 71), 0)
    shape_grad = scatter_about(key_of[2], (NF, NI, NJ), 1.0, 6.0, ((1, 32), (2, 16)), jnp.float32)
    lower_band = draw_lower_band(jax.random.fold_in(key_of[9], 71), 0)
    upper_band = draw_upper_band(jax.random.fold_in(key_of[9], 71), 0)
    jacobian = scatter_about(key_of[5], (NF, NF), NF ** -0.5, 2.5, (), jnp.float32)
    left_vectors = draw_left_vectors(jax.random.fold_in(key_of[9], 71), 0)
    right_vectors = draw_right_vectors(jax.random.fold_in(key_of[9], 71), 0)
    ctrl_local = plant(jax.random.randint(key_of[8], (NI, NJ), 0, NCTRL_SLAB), jax.random.fold_in(key_of[8], 1), 0, NCTRL_SLAB - 1).astype(jnp.int32)
    return {"adjoint": adjoint, "source": source, "shape_grad": shape_grad, "lower_band": lower_band, "upper_band": upper_band, "jacobian": jacobian, "left_vectors": left_vectors, "right_vectors": right_vectors, "ctrl_local": ctrl_local}


dissipation = 0.25
step_scale = 0.5
epsilon = 1e-06

def reference(adjoint, source, shape_grad, lower_band, upper_band, jacobian, left_vectors, right_vectors, ctrl_local):
    highest = lax.Precision.HIGHEST
    padded = jnp.pad(adjoint, ((0, 0), (1, 1), (0, 0)))
    ahead_cells = padded[:, 2:, :]
    behind = padded[:, :-2, :]
    central = jnp.einsum('fg,gij->fij', jacobian, ahead_cells - behind, precision=highest)
    residual = source - 0.5 * central + dissipation * (ahead_cells - 2.0 * adjoint + behind)
    characteristic = jnp.einsum('fg,gij->fij', left_vectors, residual, precision=highest)

    def forward_step(previous, inputs):
        rhs_cell, first_sub, second_sub = inputs
        value = rhs_cell - first_sub * previous[0] - second_sub * previous[1]
        return ((value, previous[0]), value)
    start = jnp.zeros((NF, NJ), jnp.float32)
    moved = (jnp.moveaxis(characteristic, 1, 0), jnp.moveaxis(lower_band[0], 1, 0), jnp.moveaxis(lower_band[1], 1, 0))
    _, forward = lax.scan(forward_step, (start, start), moved)

    def backward_step(previous, inputs):
        rhs_cell, diag_cell, first_sup, second_sup = inputs
        value = (rhs_cell - first_sup * previous[0] - second_sup * previous[1]) / diag_cell
        return ((value, previous[0]), value)
    moved_back = (forward, jnp.moveaxis(upper_band[0], 1, 0), jnp.moveaxis(upper_band[1], 1, 0), jnp.moveaxis(upper_band[2], 1, 0))
    _, solved = lax.scan(backward_step, (start, start), moved_back, reverse=True)
    solved = jnp.moveaxis(solved, 0, 1)
    increment = jnp.einsum('fg,gij->fij', right_vectors, solved, precision=highest)
    squares = jnp.sum(increment * increment)
    root_mean = jnp.sqrt(squares / (NF * NI * NJ) + epsilon)
    adjoint_next = adjoint + step_scale * increment / root_mean
    contribution = lax.optimization_barrier(jnp.sum(adjoint * shape_grad, axis=0))
    slab_index = (jnp.arange(NI, dtype=jnp.int32) // NI_DEV).astype(jnp.int32)
    control_point = (slab_index[:, None] * NCTRL_SLAB + ctrl_local).astype(jnp.int32)
    sensitivity = jax.ops.segment_sum(contribution.ravel(), control_point.ravel(), num_segments=NCTRL)
    return (adjoint_next, sensitivity)
```

```python
import jax
import jax.numpy as jnp
from jax import lax
from jax.experimental import pallas as pl
from jax.experimental.pallas import tpu as pltpu
from jax.sharding import PartitionSpec as P

MESH = pl.DeviceIdType.MESH
NF, CELLS = 5, 5 * 128 * 16384
NS, NC = 32, 16
dissipation = 0.25
step_scale = 0.5
epsilon = 1e-06
F32 = jnp.float32


def block_of(shape):
    return lax.broadcasted_iota(jnp.int32, shape, 1) // 32


def swap_blocks(four):
    block = block_of(four[0].shape)
    low, even = block < 2, block % 2 == 0
    a0, a1, a2, a3 = four
    m0 = pltpu.roll(jnp.where(low, a2, a0), 64, 1)
    m1 = pltpu.roll(jnp.where(low, a3, a1), 64, 1)
    x0, x2 = jnp.where(low, a0, m0), jnp.where(low, m0, a2)
    x1, x3 = jnp.where(low, a1, m1), jnp.where(low, m1, a3)
    return [
        jnp.where(even, x0, pltpu.roll(x1, 32, 1)),
        jnp.where(even, pltpu.roll(x0, 96, 1), x1),
        jnp.where(even, x2, pltpu.roll(x3, 32, 1)),
        jnp.where(even, pltpu.roll(x2, 96, 1), x3),
    ]


def mat_mul(a, b):
    return (
        a[0] * b[0] + a[1] * b[2],
        a[0] * b[1] + a[1] * b[3],
        a[2] * b[0] + a[3] * b[2],
        a[2] * b[1] + a[3] * b[3],
    )


def mat_vec(a, v):
    return (a[0] * v[0] + a[1] * v[1], a[2] * v[0] + a[3] * v[1])


def kernel(
    jac, left, right, adj_h, src_h, grad_h, low_h, up_h, ctrl_h,
    out, sens,
    adj, src, grad, low, up, ctrl, halo_s, halo_r, up_s, up_r, low_s, low_r, inc_s, inc_r,
    hot_a, hot_b, sums, cross_r, sq_s, sq_r, sq2_s, sq2_r, maps, states,
    in_sem, send_sem, recv_sem,
):
    s, c = lax.axis_index("stream"), lax.axis_index("cross")

    loads = []
    for i, (a, b) in enumerate(
        ((adj_h, adj), (up_h, up), (low_h, low), (src_h, src), (grad_h, grad), (ctrl_h, ctrl))
    ):
        copy = pltpu.make_async_copy(a, b, in_sem.at[i])
        copy.start()
        loads.append(copy)

    barrier = pltpu.get_barrier_semaphore()

    def greet_stream(k, carry):
        pl.semaphore_signal(barrier, inc=1, device_id=((s + k) % NS, c), device_id_type=MESH)
        return carry

    def greet_cross(k, carry):
        pl.semaphore_signal(barrier, inc=1, device_id=(s, (c + k) % NC), device_id_type=MESH)
        return carry

    lax.fori_loop(1, NS, greet_stream, 0)
    lax.fori_loop(1, NC, greet_cross, 0)

    def remote(a, b, n, where):
        return pltpu.make_async_remote_copy(
            src_ref=a, dst_ref=b, send_sem=send_sem.at[n], recv_sem=recv_sem.at[n],
            device_id=where, device_id_type=MESH,
        )

    def to_stream(n, source, dest):
        def body(k, carry):
            t = (s + k) % NS
            remote(source(t), dest.at[s], n, (t, c)).start()
            return carry

        lax.fori_loop(1, NS, body, 0)

    def to_cross(n, source, dest):
        def body(k, carry):
            t = (c + k) % NC
            remote(source(t), dest.at[c], n, (s, t)).start()
            return carry

        lax.fori_loop(1, NC, body, 0)

    after, before = (s + 1) % NS, (s + NS - 1) % NS

    loads[0].wait()
    halo_s[0] = adj[pl.ds(3, 40, stride=4), :]
    halo_s[1] = adj[pl.ds(0, 40, stride=4), :]
    loads[1].wait()
    for k in range(3):
        cells = [up[pl.ds(k * 160 + i, 40, stride=4), :] for i in range(4)]
        for b, packed in enumerate(swap_blocks(cells)):
            for f in range(NF):
                up_s[pl.ds(b * 16 + k * 5 + f, 8, stride=64), :] = packed[f * 8 : f * 8 + 8]

    pl.semaphore_wait(barrier, NS - 1 + NC - 1)
    behind_copy = remote(halo_s.at[0], halo_r.at[0], 0, (after, c))
    ahead_copy = remote(halo_s.at[1], halo_r.at[1], 1, (before, c))
    behind_copy.start()
    ahead_copy.start()

    def rows16(ref):
        return lambda t: ref.at[pl.ds(pl.multiple_of(t * 16, 16), 16)]

    def body_up(k, carry):
        t = (s + k) % NS
        remote(
            up_s.at[pl.ds(pl.multiple_of(t * 16, 16), 16)],
            up_r.at[pl.ds(pl.multiple_of(s * 16, 16), 16)], 2, (t, c),
        ).start()
        return carry

    lax.fori_loop(1, NS, body_up, 0)
    mine = pl.ds(pl.multiple_of(s * 16, 16), 16)
    up_r[mine, :] = up_s[mine, :]

    loads[2].wait()
    for k in range(2):
        cells = [low[pl.ds(k * 160 + i, 40, stride=4), :] for i in range(4)]
        for b, packed in enumerate(swap_blocks(cells)):
            for f in range(NF):
                low_s[pl.ds(b * 16 + k * 5 + f, 8, stride=64), :] = packed[f * 8 : f * 8 + 8]
    loads[3].wait()
    behind_copy.wait()
    ahead_copy.wait()
    own = [adj[pl.ds(i, 40, stride=4), :] for i in range(4)]
    first = jnp.where(s == 0, 0.0, halo_r[0])
    last = jnp.where(s == NS - 1, 0.0, halo_r[1])
    line = [first] + own + [last]
    characteristic = []
    for i in range(4):
        difference = line[i + 2] - line[i]
        smooth = src[pl.ds(i, 40, stride=4), :] + dissipation * (
            line[i + 2] - 2.0 * line[i + 1] + line[i]
        )
        parts = [difference[g * 8 : g * 8 + 8] for g in range(NF)]
        residual = []
        for f in range(NF):
            central = jac[f, 0] * parts[0]
            for g in range(1, NF):
                central += jac[f, g] * parts[g]
            residual.append(smooth[f * 8 : f * 8 + 8] - 0.5 * central)
        fields = []
        for f in range(NF):
            value = left[f, 0] * residual[0]
            for g in range(1, NF):
                value += left[f, g] * residual[g]
            fields.append(value)
        characteristic.append(jnp.concatenate(fields, axis=0))
    for b, packed in enumerate(swap_blocks(characteristic)):
        for f in range(NF):
            low_s[pl.ds(b * 16 + 10 + f, 8, stride=64), :] = packed[f * 8 : f * 8 + 8]

    def body_low(k, carry):
        t = (s + k) % NS
        remote(
            low_s.at[pl.ds(pl.multiple_of(t * 16, 16), 16)],
            low_r.at[pl.ds(pl.multiple_of(s * 16, 16), 16)], 3, (t, c),
        ).start()
        return carry

    lax.fori_loop(1, NS, body_low, 0)
    low_r[mine, :] = low_s[mine, :]

    loads[4].wait()
    loads[5].wait()
    terms = adj[0:32] * grad[0:32]
    for f in range(1, NF):
        terms += adj[f * 32 : f * 32 + 32] * grad[f * 32 : f * 32 + 32]
    coarse = terms.astype(jnp.bfloat16).astype(F32)
    fine = terms - coarse
    where = ctrl[...]
    high_part, low_part = where // 128, where % 128
    rows = lax.broadcasted_iota(jnp.int32, (128, 128), 0)
    for r in range(32):
        at = slice(r * 128, r * 128 + 128)
        hot_a[:, at] = jnp.where(rows == high_part[r : r + 1], 1.0, 0.0).astype(jnp.bfloat16)
        hit = rows == low_part[r : r + 1]
        hot_b[0:128, at] = jnp.where(hit, coarse[r : r + 1], 0.0).astype(jnp.bfloat16)
        hot_b[128:256, at] = jnp.where(hit, fine[r : r + 1], 0.0).astype(jnp.bfloat16)
    both = lax.dot_general(
        hot_a[...], hot_b[...], (((1,), (1,)), ((), ())), preferred_element_type=F32
    )
    sums[...] = (both[:, 0:128] + both[:, 128:256]).reshape(16, 8, 128)
    to_cross(4, lambda t: sums.at[t], cross_r)
    cross_r[c] = sums[c]

    block = block_of((40, 128))

    def unpack(ref, k):
        per_x = [
            jnp.concatenate(
                [ref[pl.ds(x * 16 + k * 5 + f, 8, stride=64), :] for f in range(NF)], axis=0
            )
            for x in range(4)
        ]
        return swap_blocks(per_x)

    def moved(values, shift, edge, fill):
        return tuple(
            jnp.where(edge, value, pltpu.roll(entry, shift, 1)) for entry, value in zip(values, fill)
        )

    unit = (1.0, 0.0, 0.0, 1.0)
    none = (0.0, 0.0)

    def prefix_mats(mats, shifts, edges):
        one = mat_mul(mats, moved(mats, shifts[0], edges[0], unit))
        two = mat_mul(one, moved(one, shifts[1], edges[1], unit))
        return one, two, moved(two, shifts[0], edges[0], unit)

    def prefix_vecs(mats, one, vecs, shifts, edges):
        moved_vecs = mat_vec(mats, moved(vecs, shifts[0], edges[0], none))
        first_vecs = tuple(a + b for a, b in zip(moved_vecs, vecs))
        moved_vecs = mat_vec(one, moved(first_vecs, shifts[1], edges[1], none))
        second = tuple(a + b for a, b in zip(moved_vecs, first_vecs))
        return second, moved(second, shifts[0], edges[0], none)

    def walk(mats, vecs, order, keep):
        for n, entry in enumerate((*mats, *vecs)):
            maps[n] = entry
        state = (jnp.zeros((NF, 128), F32),) * 2
        for z in order:
            rows_z = pl.ds(z, NF, stride=8)
            states[0, rows_z, :] = state[0]
            states[1, rows_z, :] = state[1]
            if z != order[-1]:
                at_z = [maps[n, rows_z, :] for n in range(6)]
                state = tuple(a + b for a, b in zip(mat_vec(at_z[:4], state), at_z[4:]))
        spread = []
        for n in range(2):
            value = jnp.where(block == keep, states[n], 0.0)
            value = value + pltpu.roll(value, 64, 1)
            spread.append(value + pltpu.roll(value, 32, 1))
        return spread

    def entering(mats, vecs, state):
        return tuple(a + b for a, b in zip(mat_vec(mats, state), vecs))

    def arrived(n, a, b, count, where):
        copy = remote(a.at[pl.ds(0, count)], b.at[pl.ds(0, count)], n, where)
        copy.wait()

    arrived(2, up_s, up_r, (NS - 1) * 16, (after, c))
    inverse = [1.0 / d for d in unpack(up_r, 0)]
    alpha = [u * d for u, d in zip(unpack(up_r, 1), inverse)]
    beta = [u * d for u, d in zip(unpack(up_r, 2), inverse)]
    bp, bq = [None] * 4, [None] * 4
    bp[3], bq[3] = -alpha[3], -beta[3]
    bp[2], bq[2] = -alpha[2] * bp[3] - beta[2], -alpha[2] * bq[3]
    for i in (1, 0):
        bp[i] = -alpha[i] * bp[i + 1] - beta[i] * bp[i + 2]
        bq[i] = -alpha[i] * bq[i + 1] - beta[i] * bq[i + 2]
    b_shifts, b_edges = (96, 64), (block == 3, block >= 2)
    b_mats = (bp[0], bq[0], bp[1], bq[1])
    b_one, b_two, b_before = prefix_mats(b_mats, b_shifts, b_edges)

    arrived(3, low_s, low_r, (NS - 1) * 16, (after, c))
    sub1, sub2, rhs = unpack(low_r, 0), unpack(low_r, 1), unpack(low_r, 2)
    fp, fq, fr = [-sub1[0]], [-sub2[0]], [rhs[0]]
    fp.append(-sub1[1] * fp[0] - sub2[1])
    fq.append(-sub1[1] * fq[0])
    fr.append(rhs[1] - sub1[1] * fr[0])
    for i in (2, 3):
        fp.append(-sub1[i] * fp[i - 1] - sub2[i] * fp[i - 2])
        fq.append(-sub1[i] * fq[i - 1] - sub2[i] * fq[i - 2])
        fr.append(rhs[i] - sub1[i] * fr[i - 1] - sub2[i] * fr[i - 2])
    f_shifts, f_edges = (32, 64), (block == 0, block < 2)
    f_mats = (fp[3], fq[3], fp[2], fq[2])
    f_one, f_two, f_before = prefix_mats(f_mats, f_shifts, f_edges)
    f_vecs, f_vecs_before = prefix_vecs(f_mats, f_one, (fr[3], fr[2]), f_shifts, f_edges)
    state = walk(f_two, f_vecs, list(range(8)), 3)
    enter = entering(f_before, f_vecs_before, state)
    gamma = [(fp[i] * enter[0] + fq[i] * enter[1] + fr[i]) * inverse[i] for i in range(4)]

    br = [None] * 4
    br[3] = gamma[3]
    br[2] = gamma[2] - alpha[2] * br[3]
    for i in (1, 0):
        br[i] = gamma[i] - alpha[i] * br[i + 1] - beta[i] * br[i + 2]
    b_vecs, b_vecs_before = prefix_vecs(b_mats, b_one, (br[0], br[1]), b_shifts, b_edges)
    state = walk(b_two, b_vecs, list(range(7, -1, -1)), 0)
    enter = entering(b_before, b_vecs_before, state)
    solved = [bp[i] * enter[0] + bq[i] * enter[1] + br[i] for i in range(4)]

    increment = []
    squares = jnp.zeros((8, 128), F32)
    for i in range(4):
        parts = [solved[i][g * 8 : g * 8 + 8] for g in range(NF)]
        fields = []
        for f in range(NF):
            value = right[f, 0] * parts[0]
            for g in range(1, NF):
                value += right[f, g] * parts[g]
            squares += value * value
            fields.append(value)
        increment.append(jnp.concatenate(fields, axis=0))

    sq_s[...] = jnp.broadcast_to(jnp.sum(squares, axis=0, keepdims=True), (8, 128))
    one_row = pl.ds(0, 1)

    def body_sq(k, carry):
        t = (s + k) % NS
        remote(sq_s.at[one_row], sq_r.at[s, one_row], 5, (t, c)).start()
        return carry

    lax.fori_loop(1, NS, body_sq, 0)
    sq_r[s] = sq_s[...]

    for x, packed in enumerate(swap_blocks(increment)):
        for f in range(NF):
            inc_s[pl.ds(x * 8 + f, 8, stride=32), :] = packed[f * 8 : f * 8 + 8]

    def body_inc(k, carry):
        t = (s + k) % NS
        remote(
            inc_s.at[pl.ds(pl.multiple_of(t * 8, 8), 8)],
            inc_r.at[pl.ds(pl.multiple_of(s * 8, 8), 8)], 6, (t, c),
        ).start()
        return carry

    lax.fori_loop(1, NS, body_inc, 0)
    eight = pl.ds(pl.multiple_of(s * 8, 8), 8)
    inc_r[eight, :] = inc_s[eight, :]

    def rows_arrived(n, ref, count, where):
        remote(ref.at[pl.ds(0, count), 0], ref.at[pl.ds(0, count), 0], n, where).wait()

    rows_arrived(5, sq_r, NS - 1, (after, c))
    sq2_s[...] = jnp.broadcast_to(
        jnp.sum(sq_r[:, 0, :], axis=0, keepdims=True), (8, 128)
    )

    def body_sq2(k, carry):
        t = (c + k) % NC
        remote(sq2_s.at[one_row], sq2_r.at[c, one_row], 7, (s, t)).start()
        return carry

    lax.fori_loop(1, NC, body_sq2, 0)
    sq2_r[c] = sq2_s[...]

    arrived(4, sums, cross_r, NC - 1, (s, (c + 1) % NC))
    sens[...] = jnp.sum(cross_r[...], axis=0)

    arrived(6, inc_s, inc_r, (NS - 1) * 8, (after, c))
    per_b = [
        jnp.concatenate(
            [inc_r[pl.ds(b * 8 + f, 8, stride=32), :] for f in range(NF)], axis=0
        )
        for b in range(4)
    ]
    mine_inc = swap_blocks(per_b)

    rows_arrived(7, sq2_r, NC - 1, (s, (c + 1) % NC))
    total = jnp.sum(jnp.sum(sq2_r[:, 0, :], axis=0, keepdims=True), axis=1, keepdims=True)
    scale = step_scale / jnp.sqrt(total * (1.0 / CELLS) + epsilon)
    for i in range(4):
        out[pl.ds(i, 40, stride=4), :] = own[i] + mine_inc[i] * scale


def rows_of(array):
    lead = array.shape[:-2]
    array = array.reshape(*lead, 4, 8, 128)
    return jnp.swapaxes(array, -3, -2).reshape(-1, 128)


def shards(adjoint, source, shape_grad, lower_band, upper_band, jacobian, left, right, ctrl_local):
    vmem = pltpu.VMEM
    smem = pl.BlockSpec(memory_space=pltpu.SMEM)
    hbm = pl.BlockSpec(memory_space=pl.ANY)
    out, sens = pl.pallas_call(
        kernel,
        out_shape=(jax.ShapeDtypeStruct((160, 128), F32), jax.ShapeDtypeStruct((8, 128), F32)),
        in_specs=[smem] * 3 + [hbm] * 6,
        out_specs=(pl.BlockSpec(memory_space=vmem),) * 2,
        scratch_shapes=[
            vmem((160, 128), F32),
            vmem((160, 128), F32),
            vmem((160, 128), F32),
            vmem((320, 128), F32),
            vmem((480, 128), F32),
            vmem((32, 128), jnp.int32),
            vmem((2, 40, 128), F32),
            vmem((2, 40, 128), F32),
            vmem((512, 128), F32),
            vmem((512, 128), F32),
            vmem((512, 128), F32),
            vmem((512, 128), F32),
            vmem((256, 128), F32),
            vmem((256, 128), F32),
            vmem((128, 4096), jnp.bfloat16),
            vmem((256, 4096), jnp.bfloat16),
            vmem((16, 8, 128), F32),
            vmem((16, 8, 128), F32),
            vmem((8, 128), F32),
            vmem((32, 8, 128), F32),
            vmem((8, 128), F32),
            vmem((16, 8, 128), F32),
            vmem((6, 40, 128), F32),
            vmem((2, 40, 128), F32),
            pltpu.SemaphoreType.DMA((6,)),
            pltpu.SemaphoreType.DMA((8,)),
            pltpu.SemaphoreType.DMA((8,)),
        ],
        compiler_params=pltpu.CompilerParams(
            collective_id=0, has_side_effects=True, vmem_limit_bytes=40 * 2**20
        ),
    )(
        jacobian, left, right,
        rows_of(adjoint), rows_of(source), rows_of(shape_grad), rows_of(lower_band),
        rows_of(upper_band), rows_of(ctrl_local),
    )
    adjoint_next = jnp.swapaxes(out.reshape(NF, 8, 4, 128), 1, 2).reshape(NF, 4, 1024)
    return adjoint_next, sens.reshape(1024)


def solution(mesh):
    cells = P(None, "stream", "cross")
    bands = P(None, None, "stream", "cross")
    in_specs = (cells, cells, cells, bands, bands, P(), P(), P(), P("stream", "cross"))
    out_specs = (cells, P(("stream", "cross")))
    return jax.shard_map(shards, mesh=mesh, in_specs=in_specs, out_specs=out_specs, check_vma=False)
```

```python
import jax
import jax.numpy as jnp
from jax import lax
from jax.experimental import pallas as pl
from jax.experimental.pallas import tpu as pltpu
from jax.sharding import PartitionSpec as P

MESH = pl.DeviceIdType.MESH
NF, CELLS = 5, 5 * 128 * 16384
NS, NC = 32, 16
dissipation = 0.25
step_scale = 0.5
epsilon = 1e-06
F32 = jnp.float32


def block_of(shape):
    return lax.broadcasted_iota(jnp.int32, shape, 1) // 32


def swap_blocks(four):
    block = block_of(four[0].shape)
    low, even = block < 2, block % 2 == 0
    a0, a1, a2, a3 = four
    m0 = pltpu.roll(jnp.where(low, a2, a0), 64, 1)
    m1 = pltpu.roll(jnp.where(low, a3, a1), 64, 1)
    x0, x2 = jnp.where(low, a0, m0), jnp.where(low, m0, a2)
    x1, x3 = jnp.where(low, a1, m1), jnp.where(low, m1, a3)
    return [
        jnp.where(even, x0, pltpu.roll(x1, 32, 1)),
        jnp.where(even, pltpu.roll(x0, 96, 1), x1),
        jnp.where(even, x2, pltpu.roll(x3, 32, 1)),
        jnp.where(even, pltpu.roll(x2, 96, 1), x3),
    ]


def mat_mul(a, b):
    return (
        a[0] * b[0] + a[1] * b[2],
        a[0] * b[1] + a[1] * b[3],
        a[2] * b[0] + a[3] * b[2],
        a[2] * b[1] + a[3] * b[3],
    )


def mat_vec(a, v):
    return (a[0] * v[0] + a[1] * v[1], a[2] * v[0] + a[3] * v[1])


def kernel(
    jac_h, left_h, right_h, adj_h, src_h, grad_h, low_h, up_h, ctrl_h,
    out, sens,
    jac, left, right, adj, src, grad, low, up, ctrl, halo_s, halo_r, up_s, up_r, low_s, low_r, inc_s, inc_r,
    hot_a, hot_b, sums, cross_r, sq_s, sq_r, sq2_s, sq2_r, maps, states,
    in_sem, send_sem, recv_sem,
):
    s, c = lax.axis_index("stream"), lax.axis_index("cross")

    def peer(k):
        m, n = k // 4, k % 4
        z = (s // 4 + 4 + (m + 1) // 2 * (1 - 2 * (m % 2))) % 8
        x = (s % 4 + 2 + (n + 1) // 2 * (1 - 2 * (n % 2))) % 4
        return z * 4 + x

    def cross_peer(k):
        m, n = k // 2, k % 2
        y = (c // 2 + 4 + (m + 1) // 2 * (1 - 2 * (m % 2))) % 8
        return y * 2 + (c + n + 1) % 2

    barrier = pltpu.get_barrier_semaphore()

    def greet_stream(k, carry):
        pl.semaphore_signal(barrier, inc=1, device_id=(peer(k), c), device_id_type=MESH)
        return carry

    def greet_cross(k, carry):
        pl.semaphore_signal(barrier, inc=1, device_id=(s, cross_peer(k)), device_id_type=MESH)
        return carry

    lax.fori_loop(0, NS - 1, greet_stream, 0)
    lax.fori_loop(0, NC - 1, greet_cross, 0)

    loads = []
    for i, (a, b) in enumerate(
        ((adj_h, adj), (up_h, up), (low_h, low), (src_h, src), (grad_h, grad), (ctrl_h, ctrl),
         (jac_h, jac), (left_h, left), (right_h, right))
    ):
        copy = pltpu.make_async_copy(a, b, in_sem.at[i])
        copy.start()
        loads.append(copy)

    def remote(a, b, n, where):
        return pltpu.make_async_remote_copy(
            src_ref=a, dst_ref=b, send_sem=send_sem.at[n], recv_sem=recv_sem.at[n],
            device_id=where, device_id_type=MESH,
        )

    def to_cross(n, source, dest):
        def body(k, carry):
            t = cross_peer(k)
            remote(source(t), dest.at[c], n, (s, t)).start()
            return carry

        lax.fori_loop(0, NC - 1, body, 0)

    sent = []
    after, before = (s + 1) % NS, (s + NS - 1) % NS

    loads[0].wait()
    halo_s[0] = adj[pl.ds(3, 40, stride=4), :]
    halo_s[1] = adj[pl.ds(0, 40, stride=4), :]
    loads[1].wait()
    for k in range(3):
        cells = [up[pl.ds(k * 160 + i, 40, stride=4), :] for i in range(4)]
        for b, packed in enumerate(swap_blocks(cells)):
            for f in range(NF):
                up_s[pl.ds(b * 16 + k * 5 + f, 8, stride=64), :] = packed[f * 8 : f * 8 + 8]

    pl.semaphore_wait(barrier, NS - 1 + NC - 1)
    behind_copy = remote(halo_s.at[0], halo_r.at[0], 0, (after, c))
    ahead_copy = remote(halo_s.at[1], halo_r.at[1], 1, (before, c))
    behind_copy.start()
    ahead_copy.start()

    def rows16(ref):
        return lambda t: ref.at[pl.ds(pl.multiple_of(t * 16, 16), 16)]

    def body_up(k, carry):
        t = peer(k)
        remote(
            up_s.at[pl.ds(pl.multiple_of(t * 16, 16), 15)],
            up_r.at[pl.ds(pl.multiple_of(s * 16, 16), 15)], 2, (t, c),
        ).start()
        return carry

    lax.fori_loop(0, NS - 1, body_up, 0)
    mine = pl.ds(pl.multiple_of(s * 16, 16), 16)
    up_r[mine, :] = up_s[mine, :]

    loads[2].wait()
    for k in range(2):
        cells = [low[pl.ds(k * 160 + i, 40, stride=4), :] for i in range(4)]
        for b, packed in enumerate(swap_blocks(cells)):
            for f in range(NF):
                low_s[pl.ds(b * 16 + k * 5 + f, 8, stride=64), :] = packed[f * 8 : f * 8 + 8]
    for n in (3, 6, 7, 8):
        loads[n].wait()
    behind_copy.wait_recv()
    ahead_copy.wait_recv()
    sent += [behind_copy, ahead_copy]
    own = [adj[pl.ds(i, 40, stride=4), :] for i in range(4)]
    first = jnp.where(s == 0, 0.0, halo_r[0])
    last = jnp.where(s == NS - 1, 0.0, halo_r[1])
    line = [first] + own + [last]
    characteristic = []
    for i in range(4):
        difference = line[i + 2] - line[i]
        smooth = src[pl.ds(i, 40, stride=4), :] + dissipation * (
            line[i + 2] - 2.0 * line[i + 1] + line[i]
        )
        parts = [difference[g * 8 : g * 8 + 8] for g in range(NF)]
        residual = []
        for f in range(NF):
            central = jac[f, 0] * parts[0]
            for g in range(1, NF):
                central += jac[f, g] * parts[g]
            residual.append(smooth[f * 8 : f * 8 + 8] - 0.5 * central)
        fields = []
        for f in range(NF):
            value = left[f, 0] * residual[0]
            for g in range(1, NF):
                value += left[f, g] * residual[g]
            fields.append(value)
        characteristic.append(jnp.concatenate(fields, axis=0))
    for b, packed in enumerate(swap_blocks(characteristic)):
        for f in range(NF):
            low_s[pl.ds(b * 16 + 10 + f, 8, stride=64), :] = packed[f * 8 : f * 8 + 8]

    def body_low(k, carry):
        t = peer(k)
        remote(
            low_s.at[pl.ds(pl.multiple_of(t * 16, 16), 15)],
            low_r.at[pl.ds(pl.multiple_of(s * 16, 16), 15)], 3, (t, c),
        ).start()
        return carry

    lax.fori_loop(0, NS - 1, body_low, 0)
    low_r[mine, :] = low_s[mine, :]

    loads[4].wait()
    loads[5].wait()
    terms = adj[0:32] * grad[0:32]
    for f in range(1, NF):
        terms += adj[f * 32 : f * 32 + 32] * grad[f * 32 : f * 32 + 32]
    coarse = terms.astype(jnp.bfloat16).astype(F32)
    fine = terms - coarse
    where = ctrl[...]
    high_part, low_part = where // 128, where % 128
    rows = lax.broadcasted_iota(jnp.int32, (128, 128), 0)
    for r in range(32):
        at = slice(r * 128, r * 128 + 128)
        hot_a[:, at] = jnp.where(rows == high_part[r : r + 1], 1.0, 0.0).astype(jnp.bfloat16)
        hit = rows == low_part[r : r + 1]
        hot_b[0:128, at] = jnp.where(hit, coarse[r : r + 1], 0.0).astype(jnp.bfloat16)
        hot_b[128:256, at] = jnp.where(hit, fine[r : r + 1], 0.0).astype(jnp.bfloat16)
    both = lax.dot_general(
        hot_a[...], hot_b[...], (((1,), (1,)), ((), ())), preferred_element_type=F32
    )
    sums[...] = (both[:, 0:128] + both[:, 128:256]).reshape(16, 8, 128)
    to_cross(4, lambda t: sums.at[t], cross_r)
    cross_r[c] = sums[c]

    block = block_of((40, 128))

    def unpack(ref, k):
        per_x = [
            jnp.concatenate(
                [ref[pl.ds(x * 16 + k * 5 + f, 8, stride=64), :] for f in range(NF)], axis=0
            )
            for x in range(4)
        ]
        return swap_blocks(per_x)

    def moved(values, shift, edge, fill):
        return tuple(
            jnp.where(edge, value, pltpu.roll(entry, shift, 1)) for entry, value in zip(values, fill)
        )

    unit = (1.0, 0.0, 0.0, 1.0)
    none = (0.0, 0.0)

    def prefix_mats(mats, shifts, edges):
        one = mat_mul(mats, moved(mats, shifts[0], edges[0], unit))
        two = mat_mul(one, moved(one, shifts[1], edges[1], unit))
        return one, two, moved(two, shifts[0], edges[0], unit)

    def prefix_vecs(mats, one, vecs, shifts, edges):
        moved_vecs = mat_vec(mats, moved(vecs, shifts[0], edges[0], none))
        first_vecs = tuple(a + b for a, b in zip(moved_vecs, vecs))
        moved_vecs = mat_vec(one, moved(first_vecs, shifts[1], edges[1], none))
        second = tuple(a + b for a, b in zip(moved_vecs, first_vecs))
        return second, moved(second, shifts[0], edges[0], none)

    def walk(mats, vecs, order, keep):
        for n, entry in enumerate((*mats, *vecs)):
            maps[n] = entry
        state = (jnp.zeros((NF, 128), F32),) * 2
        for z in order:
            rows_z = pl.ds(z, NF, stride=8)
            states[0, rows_z, :] = state[0]
            states[1, rows_z, :] = state[1]
            if z != order[-1]:
                at_z = [maps[n, rows_z, :] for n in range(6)]
                state = tuple(a + b for a, b in zip(mat_vec(at_z[:4], state), at_z[4:]))
        spread = []
        for n in range(2):
            value = jnp.where(block == keep, states[n], 0.0)
            value = value + pltpu.roll(value, 64, 1)
            spread.append(value + pltpu.roll(value, 32, 1))
        return spread

    def entering(mats, vecs, state):
        return tuple(a + b for a, b in zip(mat_vec(mats, state), vecs))

    def arrived(n, a, b, count, where):
        copy = remote(a.at[pl.ds(0, count)], b.at[pl.ds(0, count)], n, where)
        copy.wait_recv()
        sent.append(copy)

    arrived(2, up_s, up_r, (NS - 1) * 15, (after, c))
    inverse = [1.0 / d for d in unpack(up_r, 0)]
    alpha = [u * d for u, d in zip(unpack(up_r, 1), inverse)]
    beta = [u * d for u, d in zip(unpack(up_r, 2), inverse)]
    bp, bq = [None] * 4, [None] * 4
    bp[3], bq[3] = -alpha[3], -beta[3]
    bp[2], bq[2] = -alpha[2] * bp[3] - beta[2], -alpha[2] * bq[3]
    for i in (1, 0):
        bp[i] = -alpha[i] * bp[i + 1] - beta[i] * bp[i + 2]
        bq[i] = -alpha[i] * bq[i + 1] - beta[i] * bq[i + 2]
    b_shifts, b_edges = (96, 64), (block == 3, block >= 2)
    b_mats = (bp[0], bq[0], bp[1], bq[1])
    b_one, b_two, b_before = prefix_mats(b_mats, b_shifts, b_edges)

    arrived(3, low_s, low_r, (NS - 1) * 15, (after, c))
    sub1, sub2, rhs = unpack(low_r, 0), unpack(low_r, 1), unpack(low_r, 2)
    fp, fq, fr = [-sub1[0]], [-sub2[0]], [rhs[0]]
    fp.append(-sub1[1] * fp[0] - sub2[1])
    fq.append(-sub1[1] * fq[0])
    fr.append(rhs[1] - sub1[1] * fr[0])
    for i in (2, 3):
        fp.append(-sub1[i] * fp[i - 1] - sub2[i] * fp[i - 2])
        fq.append(-sub1[i] * fq[i - 1] - sub2[i] * fq[i - 2])
        fr.append(rhs[i] - sub1[i] * fr[i - 1] - sub2[i] * fr[i - 2])
    f_shifts, f_edges = (32, 64), (block == 0, block < 2)
    f_mats = (fp[3], fq[3], fp[2], fq[2])
    f_one, f_two, f_before = prefix_mats(f_mats, f_shifts, f_edges)
    f_vecs, f_vecs_before = prefix_vecs(f_mats, f_one, (fr[3], fr[2]), f_shifts, f_edges)
    state = walk(f_two, f_vecs, list(range(8)), 3)
    enter = entering(f_before, f_vecs_before, state)
    gamma = [(fp[i] * enter[0] + fq[i] * enter[1] + fr[i]) * inverse[i] for i in range(4)]

    br = [None] * 4
    br[3] = gamma[3]
    br[2] = gamma[2] - alpha[2] * br[3]
    for i in (1, 0):
        br[i] = gamma[i] - alpha[i] * br[i + 1] - beta[i] * br[i + 2]
    b_vecs, b_vecs_before = prefix_vecs(b_mats, b_one, (br[0], br[1]), b_shifts, b_edges)
    state = walk(b_two, b_vecs, list(range(7, -1, -1)), 0)
    enter = entering(b_before, b_vecs_before, state)
    solved = [bp[i] * enter[0] + bq[i] * enter[1] + br[i] for i in range(4)]

    increment = []
    squares = jnp.zeros((8, 128), F32)
    for i in range(4):
        parts = [solved[i][g * 8 : g * 8 + 8] for g in range(NF)]
        fields = []
        for f in range(NF):
            value = right[f, 0] * parts[0]
            for g in range(1, NF):
                value += right[f, g] * parts[g]
            squares += value * value
            fields.append(value)
        increment.append(jnp.concatenate(fields, axis=0))

    sq_s[...] = jnp.broadcast_to(jnp.sum(squares, axis=0, keepdims=True), (8, 128))
    one_row = pl.ds(0, 1)

    def body_sq(k, carry):
        t = peer(k)
        remote(sq_s.at[one_row], sq_r.at[s, one_row], 5, (t, c)).start()
        return carry

    lax.fori_loop(0, NS - 1, body_sq, 0)
    sq_r[s] = sq_s[...]

    for x, packed in enumerate(swap_blocks(increment)):
        for f in range(NF):
            inc_s[pl.ds(x * 8 + f, 8, stride=32), :] = packed[f * 8 : f * 8 + 8]

    def body_inc(k, carry):
        t = peer(k)
        remote(
            inc_s.at[pl.ds(pl.multiple_of(t * 8, 8), 8)],
            inc_r.at[pl.ds(pl.multiple_of(s * 8, 8), 8)], 6, (t, c),
        ).start()
        return carry

    lax.fori_loop(0, NS - 1, body_inc, 0)
    eight = pl.ds(pl.multiple_of(s * 8, 8), 8)
    inc_r[eight, :] = inc_s[eight, :]

    def rows_arrived(n, ref, count, where):
        copy = remote(ref.at[pl.ds(0, count), 0], ref.at[pl.ds(0, count), 0], n, where)
        copy.wait_recv()
        sent.append(copy)

    rows_arrived(5, sq_r, NS - 1, (after, c))
    sq2_s[...] = jnp.broadcast_to(
        jnp.sum(sq_r[:, 0, :], axis=0, keepdims=True), (8, 128)
    )

    def body_sq2(k, carry):
        t = cross_peer(k)
        remote(sq2_s.at[one_row], sq2_r.at[c, one_row], 7, (s, t)).start()
        return carry

    lax.fori_loop(0, NC - 1, body_sq2, 0)
    sq2_r[c] = sq2_s[...]

    arrived(4, sums, cross_r, NC - 1, (s, (c + 1) % NC))
    sens[...] = jnp.sum(cross_r[...], axis=0)

    arrived(6, inc_s, inc_r, (NS - 1) * 8, (after, c))
    per_b = [
        jnp.concatenate(
            [inc_r[pl.ds(b * 8 + f, 8, stride=32), :] for f in range(NF)], axis=0
        )
        for b in range(4)
    ]
    mine_inc = swap_blocks(per_b)

    rows_arrived(7, sq2_r, NC - 1, (s, (c + 1) % NC))
    total = jnp.sum(jnp.sum(sq2_r[:, 0, :], axis=0, keepdims=True), axis=1, keepdims=True)
    scale = step_scale / jnp.sqrt(total * (1.0 / CELLS) + epsilon)
    for i in range(4):
        out[pl.ds(i, 40, stride=4), :] = own[i] + mine_inc[i] * scale
    for copy in sent:
        copy.wait_send()


def rows_of(array):
    lead = array.shape[:-2]
    array = array.reshape(*lead, 4, 8, 128)
    return jnp.swapaxes(array, -3, -2).reshape(-1, 128)


def shards(adjoint, source, shape_grad, lower_band, upper_band, jacobian, left, right, ctrl_local):
    vmem = pltpu.VMEM
    hbm = pl.BlockSpec(memory_space=pl.ANY)
    out, sens = pl.pallas_call(
        kernel,
        out_shape=(jax.ShapeDtypeStruct((160, 128), F32), jax.ShapeDtypeStruct((8, 128), F32)),
        in_specs=[hbm] * 9,
        out_specs=(pl.BlockSpec(memory_space=vmem),) * 2,
        scratch_shapes=[
            pltpu.SMEM((NF, NF), F32),
            pltpu.SMEM((NF, NF), F32),
            pltpu.SMEM((NF, NF), F32),
            vmem((160, 128), F32),
            vmem((160, 128), F32),
            vmem((160, 128), F32),
            vmem((320, 128), F32),
            vmem((480, 128), F32),
            vmem((32, 128), jnp.int32),
            vmem((2, 40, 128), F32),
            vmem((2, 40, 128), F32),
            vmem((512, 128), F32),
            vmem((512, 128), F32),
            vmem((512, 128), F32),
            vmem((512, 128), F32),
            vmem((256, 128), F32),
            vmem((256, 128), F32),
            vmem((128, 4096), jnp.bfloat16),
            vmem((256, 4096), jnp.bfloat16),
            vmem((16, 8, 128), F32),
            vmem((16, 8, 128), F32),
            vmem((8, 128), F32),
            vmem((32, 8, 128), F32),
            vmem((8, 128), F32),
            vmem((16, 8, 128), F32),
            vmem((6, 40, 128), F32),
            vmem((2, 40, 128), F32),
            pltpu.SemaphoreType.DMA((9,)),
            pltpu.SemaphoreType.DMA((8,)),
            pltpu.SemaphoreType.DMA((8,)),
        ],
        compiler_params=pltpu.CompilerParams(
            collective_id=0, has_side_effects=True, vmem_limit_bytes=60 * 2**20
        ),
    )(
        jacobian, left, right,
        rows_of(adjoint), rows_of(source), rows_of(shape_grad), rows_of(lower_band),
        rows_of(upper_band), rows_of(ctrl_local),
    )
    adjoint_next = jnp.swapaxes(out.reshape(NF, 8, 4, 128), 1, 2).reshape(NF, 4, 1024)
    return adjoint_next, sens.reshape(1024)


def solution(mesh):
    cells = P(None, "stream", "cross")
    bands = P(None, None, "stream", "cross")
    in_specs = (cells, cells, cells, bands, bands, P(), P(), P(), P("stream", "cross"))
    out_specs = (cells, P(("stream", "cross")))
    return jax.shard_map(shards, mesh=mesh, in_specs=in_specs, out_specs=out_specs, check_vma=False)
```

```python
import jax
import jax.numpy as jnp
from jax import lax
from jax.experimental import pallas as pl
from jax.experimental.pallas import tpu as pltpu
from jax.sharding import PartitionSpec as P

MESH = pl.DeviceIdType.MESH
NF, CELLS = 5, 5 * 128 * 16384
NS, NC = 32, 16
dissipation = 0.25
step_scale = 0.5
epsilon = 1e-06
F32 = jnp.float32


def block_of(shape):
    return lax.broadcasted_iota(jnp.int32, shape, 1) // 32


def swap_blocks(four):
    block = block_of(four[0].shape)
    low, even = block < 2, block % 2 == 0
    a0, a1, a2, a3 = four
    m0 = pltpu.roll(jnp.where(low, a2, a0), 64, 1)
    m1 = pltpu.roll(jnp.where(low, a3, a1), 64, 1)
    x0, x2 = jnp.where(low, a0, m0), jnp.where(low, m0, a2)
    x1, x3 = jnp.where(low, a1, m1), jnp.where(low, m1, a3)
    return [
        jnp.where(even, x0, pltpu.roll(x1, 32, 1)),
        jnp.where(even, pltpu.roll(x0, 96, 1), x1),
        jnp.where(even, x2, pltpu.roll(x3, 32, 1)),
        jnp.where(even, pltpu.roll(x2, 96, 1), x3),
    ]


def mat_mul(a, b):
    return (
        a[0] * b[0] + a[1] * b[2],
        a[0] * b[1] + a[1] * b[3],
        a[2] * b[0] + a[3] * b[2],
        a[2] * b[1] + a[3] * b[3],
    )


def mat_vec(a, v):
    return (a[0] * v[0] + a[1] * v[1], a[2] * v[0] + a[3] * v[1])


def kernel(
    jac_h, left_h, right_h, adj_h, src_h, grad_h, low_h, up_h, ctrl_h,
    out, sens,
    jac, left, right, adj, src, grad, low, up, ctrl, next_s, next_r, last_s, last_r, up_s, up_r, low_s, low_r, inc_s, inc_r,
    hot_a, hot_b, sums, cross_r, sq_s, sq_r, sq2_s, sq2_r, maps, states,
    in_sem, send_sem, recv_sem,
):
    s, c = lax.axis_index("stream"), lax.axis_index("cross")

    def peer(k):
        m, n = k // 4, k % 4
        z = (s // 4 + 4 + (m + 1) // 2 * (1 - 2 * (m % 2))) % 8
        x = (s % 4 + 2 + (n + 1) // 2 * (1 - 2 * (n % 2))) % 4
        return z * 4 + x

    def cross_peer(k):
        m, n = k // 2, k % 2
        y = (c // 2 + 4 + (m + 1) // 2 * (1 - 2 * (m % 2))) % 8
        return y * 2 + (c + n + 1) % 2

    barrier = pltpu.get_barrier_semaphore()

    def greet_stream(k, carry):
        pl.semaphore_signal(barrier, inc=1, device_id=(peer(k), c), device_id_type=MESH)
        return carry

    def greet_cross(k, carry):
        pl.semaphore_signal(barrier, inc=1, device_id=(s, cross_peer(k)), device_id_type=MESH)
        return carry

    lax.fori_loop(0, NS - 1, greet_stream, 0)
    lax.fori_loop(0, NC - 1, greet_cross, 0)

    loads = []
    for i, (a, b) in enumerate(
        ((adj_h, adj), (up_h, up), (low_h, low), (src_h, src), (grad_h, grad), (ctrl_h, ctrl),
         (jac_h, jac), (left_h, left), (right_h, right))
    ):
        copy = pltpu.make_async_copy(a, b, in_sem.at[i])
        copy.start()
        loads.append(copy)

    def remote(a, b, n, where):
        return pltpu.make_async_remote_copy(
            src_ref=a, dst_ref=b, send_sem=send_sem.at[n], recv_sem=recv_sem.at[n],
            device_id=where, device_id_type=MESH,
        )

    def to_cross(n, source, dest):
        def body(k, carry):
            t = cross_peer(k)
            remote(source(t), dest.at[c], n, (s, t)).start()
            return carry

        lax.fori_loop(0, NC - 1, body, 0)

    sent = []
    after, before = (s + 1) % NS, (s + NS - 1) % NS

    def cell(ref, k, i):
        return ref[pl.ds(k * 160 + i, 40, stride=4), :]

    def pack(ref, k, four):
        for b, packed in enumerate(swap_blocks(four)):
            for f in range(NF):
                ref[pl.ds(b * 16 + k + f, 8, stride=64), :] = packed[f * 8 : f * 8 + 8]

    def mixed(matrix, array):
        parts = [array[g * 8 : g * 8 + 8] for g in range(NF)]
        rows = []
        for f in range(NF):
            value = matrix[f, 0] * parts[0]
            for g in range(1, NF):
                value += matrix[f, g] * parts[g]
            rows.append(value)
        return jnp.concatenate(rows, axis=0)

    loads[0].wait()
    own = [cell(adj, 0, i) for i in range(4)]
    loads[1].wait()
    diag = [cell(up, 0, i) for i in range(4)]
    next_s[0:40] = own[3]
    next_s[40:80] = diag[3]
    next_s[80:120] = diag[2]
    last_s[...] = own[0]
    inverse = [1.0 / d for d in diag]
    for k in (1, 2):
        pack(up_s, k * 5 - 5, [cell(up, k, i) * inverse[i] for i in range(4)])
    loads[2].wait()
    sub1 = [cell(low, 0, i) * inverse[i] for i in range(4)]
    sub2 = [cell(low, 1, i) * inverse[i] for i in range(4)]
    pack(
        up_s, 10, [sub1[1] * diag[0], sub1[2] * diag[1], sub1[3] * diag[2], sub2[2] * diag[0]]
    )

    pl.semaphore_wait(barrier, NS - 1 + NC - 1)
    behind_copy = remote(next_s, next_r, 0, (after, c))
    ahead_copy = remote(last_s, last_r, 1, (before, c))
    behind_copy.start()
    ahead_copy.start()

    def to_owners(n, source, dest, rows):
        def body(k, carry):
            t = peer(k)
            remote(
                source.at[pl.ds(pl.multiple_of(t * 16, 16), rows)],
                dest.at[pl.ds(pl.multiple_of(s * 16, 16), rows)], n, (t, c),
            ).start()
            return carry

        lax.fori_loop(0, NS - 1, body, 0)
        mine = pl.ds(pl.multiple_of(s * 16, 16), 16)
        dest[mine, :] = source[mine, :]

    to_owners(2, up_s, up_r, 15)

    for n in (3, 6, 7, 8):
        loads[n].wait()
    behind_copy.wait_recv()
    ahead_copy.wait_recv()
    sent += [behind_copy, ahead_copy]
    first = jnp.where(s == 0, 0.0, next_r[0:40])
    last = jnp.where(s == NS - 1, 0.0, last_r[...])
    diag1, diag2 = next_r[40:80], next_r[80:120]
    line = [first] + own + [last]
    rhs = []
    for i in range(4):
        smooth = cell(src, 0, i) + dissipation * (line[i + 2] - 2.0 * line[i + 1] + line[i])
        residual = smooth - 0.5 * mixed(jac, line[i + 2] - line[i])
        rhs.append(mixed(left, residual) * inverse[i])
    pack(low_s, 0, [sub2[3] * diag[1], rhs[1], rhs[2], rhs[0]])
    pack(low_s, 5, [sub1[0] * diag1, sub2[0] * diag2, sub2[1] * diag1, rhs[3]])
    to_owners(3, low_s, low_r, 10)

    loads[4].wait()
    loads[5].wait()
    terms = adj[0:32] * grad[0:32]
    for f in range(1, NF):
        terms += adj[f * 32 : f * 32 + 32] * grad[f * 32 : f * 32 + 32]
    coarse = terms.astype(jnp.bfloat16).astype(F32)
    fine = terms - coarse
    where = ctrl[...]
    high_part, low_part = where // 128, where % 128
    rows = lax.broadcasted_iota(jnp.int32, (128, 128), 0)
    for r in range(32):
        at = slice(r * 128, r * 128 + 128)
        hot_a[:, at] = jnp.where(rows == high_part[r : r + 1], 1.0, 0.0).astype(jnp.bfloat16)
        hit = rows == low_part[r : r + 1]
        hot_b[0:128, at] = jnp.where(hit, coarse[r : r + 1], 0.0).astype(jnp.bfloat16)
        hot_b[128:256, at] = jnp.where(hit, fine[r : r + 1], 0.0).astype(jnp.bfloat16)
    both = lax.dot_general(
        hot_a[...], hot_b[...], (((1,), (1,)), ((), ())), preferred_element_type=F32
    )
    sums[...] = (both[:, 0:128] + both[:, 128:256]).reshape(16, 8, 128)
    to_cross(4, lambda t: sums.at[t], cross_r)
    cross_r[c] = sums[c]

    block = block_of((40, 128))

    def unpack(ref, k):
        per_x = [
            jnp.concatenate(
                [ref[pl.ds(x * 16 + k * 5 + f, 8, stride=64), :] for f in range(NF)], axis=0
            )
            for x in range(4)
        ]
        return swap_blocks(per_x)

    def moved(values, shift, edge, fill):
        return tuple(
            jnp.where(edge, value, pltpu.roll(entry, shift, 1)) for entry, value in zip(values, fill)
        )

    unit = (1.0, 0.0, 0.0, 1.0)
    none = (0.0, 0.0)

    def prefix_mats(mats, shifts, edges):
        one = mat_mul(mats, moved(mats, shifts[0], edges[0], unit))
        two = mat_mul(one, moved(one, shifts[1], edges[1], unit))
        return one, two, moved(two, shifts[0], edges[0], unit)

    def prefix_vecs(mats, one, vecs, shifts, edges):
        moved_vecs = mat_vec(mats, moved(vecs, shifts[0], edges[0], none))
        first_vecs = tuple(a + b for a, b in zip(moved_vecs, vecs))
        moved_vecs = mat_vec(one, moved(first_vecs, shifts[1], edges[1], none))
        second = tuple(a + b for a, b in zip(moved_vecs, first_vecs))
        return second, moved(second, shifts[0], edges[0], none)

    def walk(mats, vecs, order, keep):
        for n, entry in enumerate((*mats, *vecs)):
            maps[n] = entry
        state = (jnp.zeros((NF, 128), F32),) * 2
        for z in order:
            rows_z = pl.ds(z, NF, stride=8)
            states[0, rows_z, :] = state[0]
            states[1, rows_z, :] = state[1]
            if z != order[-1]:
                at_z = [maps[n, rows_z, :] for n in range(6)]
                state = tuple(a + b for a, b in zip(mat_vec(at_z[:4], state), at_z[4:]))
        spread = []
        for n in range(2):
            value = jnp.where(block == keep, states[n], 0.0)
            value = value + pltpu.roll(value, 64, 1)
            spread.append(value + pltpu.roll(value, 32, 1))
        return spread

    def entering(mats, vecs, state):
        return tuple(a + b for a, b in zip(mat_vec(mats, state), vecs))

    def arrived(n, a, b, count, where):
        copy = remote(a.at[pl.ds(0, count)], b.at[pl.ds(0, count)], n, where)
        copy.wait_recv()
        sent.append(copy)

    arrived(2, up_s, up_r, (NS - 1) * 15, (after, c))
    alpha, beta = unpack(up_r, 0), unpack(up_r, 1)
    sub1, sub2 = [None] * 4, [None] * 4
    sub1[1], sub1[2], sub1[3], sub2[2] = unpack(up_r, 2)
    bp, bq = [None] * 4, [None] * 4
    bp[3], bq[3] = -alpha[3], -beta[3]
    bp[2], bq[2] = -alpha[2] * bp[3] - beta[2], -alpha[2] * bq[3]
    for i in (1, 0):
        bp[i] = -alpha[i] * bp[i + 1] - beta[i] * bp[i + 2]
        bq[i] = -alpha[i] * bq[i + 1] - beta[i] * bq[i + 2]
    b_shifts, b_edges = (96, 64), (block == 3, block >= 2)
    b_mats = (bp[0], bq[0], bp[1], bq[1])
    b_one, b_two, b_before = prefix_mats(b_mats, b_shifts, b_edges)

    arrived(3, low_s, low_r, (NS - 1) * 10, (after, c))
    rhs = [None] * 4
    sub2[3], rhs[1], rhs[2], rhs[0] = unpack(low_r, 0)
    sub1[0], sub2[0], sub2[1], rhs[3] = unpack(low_r, 1)
    fp, fq, fr = [-sub1[0]], [-sub2[0]], [rhs[0]]
    fp.append(-sub1[1] * fp[0] - sub2[1])
    fq.append(-sub1[1] * fq[0])
    fr.append(rhs[1] - sub1[1] * fr[0])
    for i in (2, 3):
        fp.append(-sub1[i] * fp[i - 1] - sub2[i] * fp[i - 2])
        fq.append(-sub1[i] * fq[i - 1] - sub2[i] * fq[i - 2])
        fr.append(rhs[i] - sub1[i] * fr[i - 1] - sub2[i] * fr[i - 2])
    f_shifts, f_edges = (32, 64), (block == 0, block < 2)
    f_mats = (fp[3], fq[3], fp[2], fq[2])
    f_one, f_two, f_before = prefix_mats(f_mats, f_shifts, f_edges)
    f_vecs, f_vecs_before = prefix_vecs(f_mats, f_one, (fr[3], fr[2]), f_shifts, f_edges)
    state = walk(f_two, f_vecs, list(range(8)), 3)
    enter = entering(f_before, f_vecs_before, state)
    gamma = [fp[i] * enter[0] + fq[i] * enter[1] + fr[i] for i in range(4)]

    br = [None] * 4
    br[3] = gamma[3]
    br[2] = gamma[2] - alpha[2] * br[3]
    for i in (1, 0):
        br[i] = gamma[i] - alpha[i] * br[i + 1] - beta[i] * br[i + 2]
    b_vecs, b_vecs_before = prefix_vecs(b_mats, b_one, (br[0], br[1]), b_shifts, b_edges)
    state = walk(b_two, b_vecs, list(range(7, -1, -1)), 0)
    enter = entering(b_before, b_vecs_before, state)
    solved = [bp[i] * enter[0] + bq[i] * enter[1] + br[i] for i in range(4)]

    increment = [mixed(right, entry) for entry in solved]
    squares = sum(entry * entry for entry in increment)
    squares = sum(squares[f * 8 : f * 8 + 8] for f in range(NF))

    sq_s[...] = jnp.broadcast_to(jnp.sum(squares, axis=0, keepdims=True), (8, 128))
    one_row = pl.ds(0, 1)

    def body_sq(k, carry):
        t = peer(k)
        remote(sq_s.at[one_row], sq_r.at[s, one_row], 5, (t, c)).start()
        return carry

    lax.fori_loop(0, NS - 1, body_sq, 0)
    sq_r[s] = sq_s[...]

    for x, packed in enumerate(swap_blocks(increment)):
        for f in range(NF):
            inc_s[pl.ds(x * 8 + f, 8, stride=32), :] = packed[f * 8 : f * 8 + 8]

    def body_inc(k, carry):
        t = peer(k)
        remote(
            inc_s.at[pl.ds(pl.multiple_of(t * 8, 8), 8)],
            inc_r.at[pl.ds(pl.multiple_of(s * 8, 8), 8)], 6, (t, c),
        ).start()
        return carry

    lax.fori_loop(0, NS - 1, body_inc, 0)
    eight = pl.ds(pl.multiple_of(s * 8, 8), 8)
    inc_r[eight, :] = inc_s[eight, :]

    def rows_arrived(n, ref, count, where):
        copy = remote(ref.at[pl.ds(0, count), 0], ref.at[pl.ds(0, count), 0], n, where)
        copy.wait_recv()
        sent.append(copy)

    rows_arrived(5, sq_r, NS - 1, (after, c))
    sq2_s[...] = jnp.broadcast_to(
        jnp.sum(sq_r[:, 0, :], axis=0, keepdims=True), (8, 128)
    )

    def body_sq2(k, carry):
        t = cross_peer(k)
        remote(sq2_s.at[one_row], sq2_r.at[c, one_row], 7, (s, t)).start()
        return carry

    lax.fori_loop(0, NC - 1, body_sq2, 0)
    sq2_r[c] = sq2_s[...]

    arrived(4, sums, cross_r, NC - 1, (s, (c + 1) % NC))
    sens[...] = jnp.sum(cross_r[...], axis=0)

    arrived(6, inc_s, inc_r, (NS - 1) * 8, (after, c))
    per_b = [
        jnp.concatenate(
            [inc_r[pl.ds(b * 8 + f, 8, stride=32), :] for f in range(NF)], axis=0
        )
        for b in range(4)
    ]
    mine_inc = swap_blocks(per_b)

    rows_arrived(7, sq2_r, NC - 1, (s, (c + 1) % NC))
    total = jnp.sum(jnp.sum(sq2_r[:, 0, :], axis=0, keepdims=True), axis=1, keepdims=True)
    scale = step_scale / jnp.sqrt(total * (1.0 / CELLS) + epsilon)
    for i in range(4):
        out[pl.ds(i, 40, stride=4), :] = own[i] + mine_inc[i] * scale
    for copy in sent:
        copy.wait_send()


def rows_of(array):
    lead = array.shape[:-2]
    array = array.reshape(*lead, 4, 8, 128)
    return jnp.swapaxes(array, -3, -2).reshape(-1, 128)


def shards(adjoint, source, shape_grad, lower_band, upper_band, jacobian, left, right, ctrl_local):
    vmem = pltpu.VMEM
    hbm = pl.BlockSpec(memory_space=pl.ANY)
    out, sens = pl.pallas_call(
        kernel,
        out_shape=(jax.ShapeDtypeStruct((160, 128), F32), jax.ShapeDtypeStruct((8, 128), F32)),
        in_specs=[hbm] * 9,
        out_specs=(pl.BlockSpec(memory_space=vmem),) * 2,
        scratch_shapes=[
            pltpu.SMEM((NF, NF), F32),
            pltpu.SMEM((NF, NF), F32),
            pltpu.SMEM((NF, NF), F32),
            vmem((160, 128), F32),
            vmem((160, 128), F32),
            vmem((160, 128), F32),
            vmem((320, 128), F32),
            vmem((480, 128), F32),
            vmem((32, 128), jnp.int32),
            vmem((120, 128), F32),
            vmem((120, 128), F32),
            vmem((40, 128), F32),
            vmem((40, 128), F32),
            vmem((512, 128), F32),
            vmem((512, 128), F32),
            vmem((512, 128), F32),
            vmem((512, 128), F32),
            vmem((256, 128), F32),
            vmem((256, 128), F32),
            vmem((128, 4096), jnp.bfloat16),
            vmem((256, 4096), jnp.bfloat16),
            vmem((16, 8, 128), F32),
            vmem((16, 8, 128), F32),
            vmem((8, 128), F32),
            vmem((32, 8, 128), F32),
            vmem((8, 128), F32),
            vmem((16, 8, 128), F32),
            vmem((6, 40, 128), F32),
            vmem((2, 40, 128), F32),
            pltpu.SemaphoreType.DMA((9,)),
            pltpu.SemaphoreType.DMA((8,)),
            pltpu.SemaphoreType.DMA((8,)),
        ],
        compiler_params=pltpu.CompilerParams(
            collective_id=0, has_side_effects=True, vmem_limit_bytes=60 * 2**20
        ),
    )(
        jacobian, left, right,
        rows_of(adjoint), rows_of(source), rows_of(shape_grad), rows_of(lower_band),
        rows_of(upper_band), rows_of(ctrl_local),
    )
    adjoint_next = jnp.swapaxes(out.reshape(NF, 8, 4, 128), 1, 2).reshape(NF, 4, 1024)
    return adjoint_next, sens.reshape(1024)


def solution(mesh):
    cells = P(None, "stream", "cross")
    bands = P(None, None, "stream", "cross")
    in_specs = (cells, cells, cells, bands, bands, P(), P(), P(), P("stream", "cross"))
    out_specs = (cells, P(("stream", "cross")))
    return jax.shard_map(shards, mesh=mesh, in_specs=in_specs, out_specs=out_specs, check_vma=False)
```

```python
import jax
import jax.numpy as jnp
from jax import lax
from jax.experimental import pallas as pl
from jax.experimental.pallas import tpu as pltpu
from jax.sharding import PartitionSpec as P

MESH = pl.DeviceIdType.MESH
NF, CELLS = 5, 5 * 128 * 16384
NS, NC = 32, 16
dissipation = 0.25
step_scale = 0.5
epsilon = 1e-06
F32 = jnp.float32


def block_of(shape):
    return lax.broadcasted_iota(jnp.int32, shape, 1) // 32


def swap_blocks(four):
    block = block_of(four[0].shape)
    low, even = block < 2, block % 2 == 0
    a0, a1, a2, a3 = four
    m0 = pltpu.roll(jnp.where(low, a2, a0), 64, 1)
    m1 = pltpu.roll(jnp.where(low, a3, a1), 64, 1)
    x0, x2 = jnp.where(low, a0, m0), jnp.where(low, m0, a2)
    x1, x3 = jnp.where(low, a1, m1), jnp.where(low, m1, a3)
    return [
        jnp.where(even, x0, pltpu.roll(x1, 32, 1)),
        jnp.where(even, pltpu.roll(x0, 96, 1), x1),
        jnp.where(even, x2, pltpu.roll(x3, 32, 1)),
        jnp.where(even, pltpu.roll(x2, 96, 1), x3),
    ]


def mat_mul(a, b):
    return (
        a[0] * b[0] + a[1] * b[2],
        a[0] * b[1] + a[1] * b[3],
        a[2] * b[0] + a[3] * b[2],
        a[2] * b[1] + a[3] * b[3],
    )


def mat_vec(a, v):
    return (a[0] * v[0] + a[1] * v[1], a[2] * v[0] + a[3] * v[1])


def kernel(
    jac_h, left_h, right_h, adj_h, src_h, grad_h, low_h, up_h, ctrl_h,
    out, sens,
    jac, left, right, adj, src, grad, low, up, ctrl, next_s, next_r, last_s, last_r, up_s, up_r, low_s, low_r, inc_s, inc_r,
    hot_a, hot_b, sums, cross_r, sq_s, sq_r, sq2_s, sq2_r, maps, states,
    in_sem, send_sem, recv_sem,
):
    s, c = lax.axis_index("stream"), lax.axis_index("cross")

    def peer(k):
        m, n = k // 4, k % 4
        z = (s // 4 + 4 + (m + 1) // 2 * (1 - 2 * (m % 2))) % 8
        x = (s % 4 + 2 + (n + 1) // 2 * (1 - 2 * (n % 2))) % 4
        return z * 4 + x

    def cross_peer(k):
        m, n = k // 2, k % 2
        y = (c // 2 + 4 + (m + 1) // 2 * (1 - 2 * (m % 2))) % 8
        return y * 2 + (c + n + 1) % 2

    barrier = pltpu.get_barrier_semaphore()

    def greet_stream(k, carry):
        pl.semaphore_signal(barrier, inc=1, device_id=(peer(k), c), device_id_type=MESH)
        return carry

    def greet_cross(k, carry):
        pl.semaphore_signal(barrier, inc=1, device_id=(s, cross_peer(k)), device_id_type=MESH)
        return carry

    lax.fori_loop(0, NS - 1, greet_stream, 0)
    lax.fori_loop(0, NC - 1, greet_cross, 0)

    loads = []
    for i, (a, b) in enumerate(
        ((adj_h, adj), (up_h, up), (low_h, low), (src_h, src), (grad_h, grad), (ctrl_h, ctrl),
         (jac_h, jac), (left_h, left), (right_h, right))
    ):
        copy = pltpu.make_async_copy(a, b, in_sem.at[i])
        copy.start()
        loads.append(copy)

    def remote(a, b, n, where):
        return pltpu.make_async_remote_copy(
            src_ref=a, dst_ref=b, send_sem=send_sem.at[n], recv_sem=recv_sem.at[n],
            device_id=where, device_id_type=MESH,
        )

    def to_cross(n, source, dest):
        def body(k, carry):
            t = cross_peer(k)
            remote(source(t), dest.at[c], n, (s, t)).start()
            return carry

        lax.fori_loop(0, NC - 1, body, 0)

    sent = []
    after, before = (s + 1) % NS, (s + NS - 1) % NS

    def cell(ref, k, i):
        return ref[pl.ds(k * 160 + i, 40, stride=4), :]

    def pack(ref, k, four):
        for b, packed in enumerate(swap_blocks(four)):
            for f in range(NF):
                ref[pl.ds(b * 16 + k + f, 8, stride=64), :] = packed[f * 8 : f * 8 + 8]

    def mixed(matrix, array):
        parts = [array[g * 8 : g * 8 + 8] for g in range(NF)]
        rows = []
        for f in range(NF):
            value = matrix[f, 0] * parts[0]
            for g in range(1, NF):
                value += matrix[f, g] * parts[g]
            rows.append(value)
        return jnp.concatenate(rows, axis=0)

    loads[0].wait()
    own = [cell(adj, 0, i) for i in range(4)]
    loads[1].wait()
    diag = [cell(up, 0, i) for i in range(4)]
    next_s[0:40] = own[3]
    next_s[40:80] = diag[3]
    next_s[80:120] = diag[2]
    last_s[...] = own[0]
    inverse = [1.0 / d for d in diag]
    for k in (1, 2):
        pack(up_s, k * 5 - 5, [cell(up, k, i) * inverse[i] for i in range(4)])
    loads[2].wait()
    sub1 = [cell(low, 0, i) * inverse[i] for i in range(4)]
    sub2 = [cell(low, 1, i) * inverse[i] for i in range(4)]
    pack(
        up_s, 10, [sub1[1] * diag[0], sub1[2] * diag[1], sub1[3] * diag[2], sub2[2] * diag[0]]
    )

    pl.semaphore_wait(barrier, NS - 1 + NC - 1)
    behind_copy = remote(next_s, next_r, 0, (after, c))
    ahead_copy = remote(last_s, last_r, 1, (before, c))
    behind_copy.start()
    ahead_copy.start()

    def to_owners(n, source, dest, rows):
        def body(k, carry):
            t = peer(k)
            remote(
                source.at[pl.ds(pl.multiple_of(t * 16, 16), rows)],
                dest.at[pl.ds(pl.multiple_of(s * 16, 16), rows)], n, (t, c),
            ).start()
            return carry

        lax.fori_loop(0, NS - 1, body, 0)
        mine = pl.ds(pl.multiple_of(s * 16, 16), 16)
        dest[mine, :] = source[mine, :]

    to_owners(2, up_s, up_r, 15)

    for n in (3, 6, 7, 8):
        loads[n].wait()
    behind_copy.wait_recv()
    ahead_copy.wait_recv()
    sent += [behind_copy, ahead_copy]
    first = jnp.where(s == 0, 0.0, next_r[0:40])
    last = jnp.where(s == NS - 1, 0.0, last_r[...])
    diag1, diag2 = next_r[40:80], next_r[80:120]
    line = [first] + own + [last]
    rhs = []
    for i in range(4):
        smooth = cell(src, 0, i) + dissipation * (line[i + 2] - 2.0 * line[i + 1] + line[i])
        residual = smooth - 0.5 * mixed(jac, line[i + 2] - line[i])
        rhs.append(mixed(left, residual) * inverse[i])
    pack(low_s, 0, [sub2[3] * diag[1], rhs[1], rhs[2], rhs[0]])
    pack(low_s, 5, [sub1[0] * diag1, sub2[0] * diag2, sub2[1] * diag1, rhs[3]])
    to_owners(3, low_s, low_r, 10)

    loads[4].wait()
    loads[5].wait()
    terms = adj[0:32] * grad[0:32]
    for f in range(1, NF):
        terms += adj[f * 32 : f * 32 + 32] * grad[f * 32 : f * 32 + 32]
    coarse = terms.astype(jnp.bfloat16).astype(F32)
    fine = terms - coarse
    where = ctrl[...]
    high_part, low_part = where // 128, where % 128
    rows = lax.broadcasted_iota(jnp.int32, (128, 128), 0)
    for r in range(32):
        at = slice(r * 128, r * 128 + 128)
        hot_a[:, at] = jnp.where(rows == high_part[r : r + 1], 1.0, 0.0).astype(jnp.bfloat16)
        hit = rows == low_part[r : r + 1]
        hot_b[0:128, at] = jnp.where(hit, coarse[r : r + 1], 0.0).astype(jnp.bfloat16)
        hot_b[128:256, at] = jnp.where(hit, fine[r : r + 1], 0.0).astype(jnp.bfloat16)
    both = lax.dot_general(
        hot_a[...], hot_b[...], (((1,), (1,)), ((), ())), preferred_element_type=F32
    )
    sums[...] = (both[:, 0:128] + both[:, 128:256]).reshape(16, 8, 128)
    to_cross(4, lambda t: sums.at[t], cross_r)
    cross_r[c] = sums[c]

    block = block_of((40, 128))

    def unpack(ref, k):
        per_x = [
            jnp.concatenate(
                [ref[pl.ds(x * 16 + k * 5 + f, 8, stride=64), :] for f in range(NF)], axis=0
            )
            for x in range(4)
        ]
        return swap_blocks(per_x)

    def moved(values, shift, edge, fill):
        return tuple(
            jnp.where(edge, value, pltpu.roll(entry, shift, 1)) for entry, value in zip(values, fill)
        )

    unit = (1.0, 0.0, 0.0, 1.0)
    none = (0.0, 0.0)

    def prefix_mats(mats, shifts, edges):
        one = mat_mul(mats, moved(mats, shifts[0], edges[0], unit))
        two = mat_mul(one, moved(one, shifts[1], edges[1], unit))
        return one, two, moved(two, shifts[0], edges[0], unit)

    def prefix_vecs(mats, one, vecs, shifts, edges):
        moved_vecs = mat_vec(mats, moved(vecs, shifts[0], edges[0], none))
        first_vecs = tuple(a + b for a, b in zip(moved_vecs, vecs))
        moved_vecs = mat_vec(one, moved(first_vecs, shifts[1], edges[1], none))
        second = tuple(a + b for a, b in zip(moved_vecs, first_vecs))
        return second, moved(second, shifts[0], edges[0], none)

    def walk(mats, vecs, order, keep):
        for n, entry in enumerate((*mats, *vecs)):
            maps[n] = entry
        state = (jnp.zeros((NF, 128), F32),) * 2
        for z in order:
            rows_z = pl.ds(z, NF, stride=8)
            states[0, rows_z, :] = state[0]
            states[1, rows_z, :] = state[1]
            if z != order[-1]:
                at_z = [maps[n, rows_z, :] for n in range(6)]
                state = tuple(a + b for a, b in zip(mat_vec(at_z[:4], state), at_z[4:]))
        spread = []
        for n in range(2):
            value = jnp.where(block == keep, states[n], 0.0)
            value = value + pltpu.roll(value, 64, 1)
            spread.append(value + pltpu.roll(value, 32, 1))
        return spread

    def entering(mats, vecs, state):
        return tuple(a + b for a, b in zip(mat_vec(mats, state), vecs))

    def arrived(n, a, b, count, where):
        copy = remote(a.at[pl.ds(0, count)], b.at[pl.ds(0, count)], n, where)
        copy.wait_recv()
        sent.append(copy)

    arrived(2, up_s, up_r, (NS - 1) * 15, (after, c))
    alpha, beta = unpack(up_r, 0), unpack(up_r, 1)
    sub1, sub2 = [None] * 4, [None] * 4
    sub1[1], sub1[2], sub1[3], sub2[2] = unpack(up_r, 2)
    bp, bq = [None] * 4, [None] * 4
    bp[3], bq[3] = -alpha[3], -beta[3]
    bp[2], bq[2] = -alpha[2] * bp[3] - beta[2], -alpha[2] * bq[3]
    for i in (1, 0):
        bp[i] = -alpha[i] * bp[i + 1] - beta[i] * bp[i + 2]
        bq[i] = -alpha[i] * bq[i + 1] - beta[i] * bq[i + 2]
    b_shifts, b_edges = (96, 64), (block == 3, block >= 2)
    b_mats = (bp[0], bq[0], bp[1], bq[1])
    b_one, b_two, b_before = prefix_mats(b_mats, b_shifts, b_edges)

    arrived(3, low_s, low_r, (NS - 1) * 10, (after, c))
    rhs = [None] * 4
    sub2[3], rhs[1], rhs[2], rhs[0] = unpack(low_r, 0)
    sub1[0], sub2[0], sub2[1], rhs[3] = unpack(low_r, 1)
    fp, fq, fr = [-sub1[0]], [-sub2[0]], [rhs[0]]
    fp.append(-sub1[1] * fp[0] - sub2[1])
    fq.append(-sub1[1] * fq[0])
    fr.append(rhs[1] - sub1[1] * fr[0])
    for i in (2, 3):
        fp.append(-sub1[i] * fp[i - 1] - sub2[i] * fp[i - 2])
        fq.append(-sub1[i] * fq[i - 1] - sub2[i] * fq[i - 2])
        fr.append(rhs[i] - sub1[i] * fr[i - 1] - sub2[i] * fr[i - 2])
    f_shifts, f_edges = (32, 64), (block == 0, block < 2)
    f_mats = (fp[3], fq[3], fp[2], fq[2])
    f_one, f_two, f_before = prefix_mats(f_mats, f_shifts, f_edges)
    f_vecs, f_vecs_before = prefix_vecs(f_mats, f_one, (fr[3], fr[2]), f_shifts, f_edges)
    state = walk(f_two, f_vecs, list(range(8)), 3)
    enter = entering(f_before, f_vecs_before, state)
    gamma = [fp[i] * enter[0] + fq[i] * enter[1] + fr[i] for i in range(4)]

    br = [None] * 4
    br[3] = gamma[3]
    br[2] = gamma[2] - alpha[2] * br[3]
    for i in (1, 0):
        br[i] = gamma[i] - alpha[i] * br[i + 1] - beta[i] * br[i + 2]
    b_vecs, b_vecs_before = prefix_vecs(b_mats, b_one, (br[0], br[1]), b_shifts, b_edges)
    state = walk(b_two, b_vecs, list(range(7, -1, -1)), 0)
    enter = entering(b_before, b_vecs_before, state)
    solved = [bp[i] * enter[0] + bq[i] * enter[1] + br[i] for i in range(4)]

    increment = [mixed(right, entry) for entry in solved]
    squares = sum(entry * entry for entry in increment)
    squares = sum(squares[f * 8 : f * 8 + 8] for f in range(NF))

    sq_s[...] = jnp.broadcast_to(jnp.sum(squares, axis=0, keepdims=True), (8, 128))
    one_row = pl.ds(0, 1)

    def body_sq(k, carry):
        t = peer(k)
        remote(sq_s.at[one_row], sq_r.at[s, one_row], 5, (t, c)).start()
        return carry

    lax.fori_loop(0, NS - 1, body_sq, 0)
    sq_r[s] = sq_s[...]

    for x, packed in enumerate(swap_blocks(increment)):
        for f in range(NF):
            inc_s[pl.ds(x * 8 + f, 8, stride=32), :] = packed[f * 8 : f * 8 + 8]

    def body_inc(k, carry):
        t = peer(k)
        remote(
            inc_s.at[pl.ds(pl.multiple_of(t * 8, 8), 8)],
            inc_r.at[pl.ds(pl.multiple_of(s * 8, 8), 8)], 6, (t, c),
        ).start()
        return carry

    lax.fori_loop(0, NS - 1, body_inc, 0)
    eight = pl.ds(pl.multiple_of(s * 8, 8), 8)
    inc_r[eight, :] = inc_s[eight, :]

    def rows_arrived(n, ref, count, where):
        copy = remote(ref.at[pl.ds(0, count), 0], ref.at[pl.ds(0, count), 0], n, where)
        copy.wait_recv()
        sent.append(copy)

    rows_arrived(5, sq_r, NS - 1, (after, c))
    sq2_s[...] = jnp.broadcast_to(
        jnp.sum(sq_r[:, 0, :], axis=0, keepdims=True), (8, 128)
    )

    def body_sq2(k, carry):
        t = cross_peer(k)
        remote(sq2_s.at[one_row], sq2_r.at[c, one_row], 7, (s, t)).start()
        return carry

    lax.fori_loop(0, NC - 1, body_sq2, 0)
    sq2_r[c] = sq2_s[...]

    arrived(4, sums, cross_r, NC - 1, (s, (c + 1) % NC))
    sens[...] = jnp.sum(cross_r[...], axis=0)

    arrived(6, inc_s, inc_r, (NS - 1) * 8, (after, c))
    per_b = [
        jnp.concatenate(
            [inc_r[pl.ds(b * 8 + f, 8, stride=32), :] for f in range(NF)], axis=0
        )
        for b in range(4)
    ]
    mine_inc = swap_blocks(per_b)

    rows_arrived(7, sq2_r, NC - 1, (s, (c + 1) % NC))
    total = jnp.sum(jnp.sum(sq2_r[:, 0, :], axis=0, keepdims=True), axis=1, keepdims=True)
    scale = step_scale / jnp.sqrt(total * (1.0 / CELLS) + epsilon)
    for i in range(4):
        out[pl.ds(i, 40, stride=4), :] = own[i] + mine_inc[i] * scale
    for copy in sent:
        copy.wait_send()


def rows_of(array):
    lead = array.shape[:-2]
    array = array.reshape(*lead, 4, 8, 128)
    return jnp.swapaxes(array, -3, -2).reshape(-1, 128)


def shards(adjoint, source, shape_grad, lower_band, upper_band, jacobian, left, right, ctrl_local):
    vmem = pltpu.VMEM
    hbm = pl.BlockSpec(memory_space=pl.ANY)
    out, sens = pl.pallas_call(
        kernel,
        out_shape=(jax.ShapeDtypeStruct((160, 128), F32), jax.ShapeDtypeStruct((8, 128), F32)),
        in_specs=[hbm] * 9,
        out_specs=(pl.BlockSpec(memory_space=vmem),) * 2,
        scratch_shapes=[
            pltpu.SMEM((NF, NF), F32),
            pltpu.SMEM((NF, NF), F32),
            pltpu.SMEM((NF, NF), F32),
            vmem((160, 128), F32),
            vmem((160, 128), F32),
            vmem((160, 128), F32),
            vmem((320, 128), F32),
            vmem((480, 128), F32),
            vmem((32, 128), jnp.int32),
            vmem((120, 128), F32),
            vmem((120, 128), F32),
            vmem((40, 128), F32),
            vmem((40, 128), F32),
            vmem((512, 128), F32),
            vmem((512, 128), F32),
            vmem((512, 128), F32),
            vmem((512, 128), F32),
            vmem((256, 128), F32),
            vmem((256, 128), F32),
            vmem((128, 4096), jnp.bfloat16),
            vmem((256, 4096), jnp.bfloat16),
            vmem((16, 8, 128), F32),
            vmem((16, 8, 128), F32),
            vmem((8, 128), F32),
            vmem((32, 8, 128), F32),
            vmem((8, 128), F32),
            vmem((16, 8, 128), F32),
            vmem((6, 40, 128), F32),
            vmem((2, 40, 128), F32),
            pltpu.SemaphoreType.DMA((9,)),
            pltpu.SemaphoreType.DMA((8,)),
            pltpu.SemaphoreType.DMA((8,)),
        ],
        compiler_params=pltpu.CompilerParams(
            collective_id=0, has_side_effects=True, vmem_limit_bytes=40 * 2**20
        ),
    )(
        *(pltpu.with_memory_space_constraint(x, pltpu.HBM) for x in (
        jacobian, left, right,
        rows_of(adjoint), rows_of(source), rows_of(shape_grad), rows_of(lower_band),
        rows_of(upper_band), rows_of(ctrl_local)))
    )
    adjoint_next = jnp.swapaxes(out.reshape(NF, 8, 4, 128), 1, 2).reshape(NF, 4, 1024)
    return adjoint_next, sens.reshape(1024)


def solution(mesh):
    cells = P(None, "stream", "cross")
    bands = P(None, None, "stream", "cross")
    in_specs = (cells, cells, cells, bands, bands, P(), P(), P(), P("stream", "cross"))
    out_specs = (cells, P(("stream", "cross")))
    return jax.shard_map(shards, mesh=mesh, in_specs=in_specs, out_specs=out_specs, check_vma=False)
```

```python
import jax
import jax.numpy as jnp
from jax import lax
from jax.experimental import pallas as pl
from jax.experimental.pallas import tpu as pltpu
from jax.sharding import PartitionSpec as P

MESH = pl.DeviceIdType.MESH
NF, CELLS = 5, 5 * 128 * 16384
NS, NC = 32, 16
dissipation = 0.25
step_scale = 0.5
epsilon = 1e-06
F32 = jnp.float32


def block_of(shape):
    return lax.broadcasted_iota(jnp.int32, shape, 1) // 32


def swap_blocks(four):
    block = block_of(four[0].shape)
    low, even = block < 2, block % 2 == 0
    a0, a1, a2, a3 = four
    m0 = pltpu.roll(jnp.where(low, a2, a0), 64, 1)
    m1 = pltpu.roll(jnp.where(low, a3, a1), 64, 1)
    x0, x2 = jnp.where(low, a0, m0), jnp.where(low, m0, a2)
    x1, x3 = jnp.where(low, a1, m1), jnp.where(low, m1, a3)
    return [
        jnp.where(even, x0, pltpu.roll(x1, 32, 1)),
        jnp.where(even, pltpu.roll(x0, 96, 1), x1),
        jnp.where(even, x2, pltpu.roll(x3, 32, 1)),
        jnp.where(even, pltpu.roll(x2, 96, 1), x3),
    ]


def mat_mul(a, b):
    return (
        a[0] * b[0] + a[1] * b[2],
        a[0] * b[1] + a[1] * b[3],
        a[2] * b[0] + a[3] * b[2],
        a[2] * b[1] + a[3] * b[3],
    )


def mat_vec(a, v):
    return (a[0] * v[0] + a[1] * v[1], a[2] * v[0] + a[3] * v[1])


def kernel(
    jac_h, left_h, right_h, adj_h, src_h, grad_h, low_h, up_h, ctrl_h,
    out, sens,
    jac, left, right, adj, src, grad, low, up, ctrl, next_s, next_r, last_s, last_r, up_s, up_r, low_s, low_r, inc_s, inc_r,
    hot_a, hot_b, sums, cross_r, sq_s, sq_r, sq2_s, sq2_r, maps, states,
    in_sem, send_sem, recv_sem,
):
    s, c = lax.axis_index("stream"), lax.axis_index("cross")

    def peer(k):
        m, n = k // 4, k % 4
        z = (s // 4 + 4 + (m + 1) // 2 * (1 - 2 * (m % 2))) % 8
        x = (s % 4 + 2 + (n + 1) // 2 * (1 - 2 * (n % 2))) % 4
        return z * 4 + x

    def cross_peer(k):
        m, n = k // 2, k % 2
        y = (c // 2 + 4 + (m + 1) // 2 * (1 - 2 * (m % 2))) % 8
        return y * 2 + (c + n + 1) % 2

    barrier = pltpu.get_barrier_semaphore()

    def greet_stream(k, carry):
        pl.semaphore_signal(barrier, inc=1, device_id=(peer(k), c), device_id_type=MESH)
        return carry

    def greet_cross(k, carry):
        pl.semaphore_signal(barrier, inc=1, device_id=(s, cross_peer(k)), device_id_type=MESH)
        return carry

    lax.fori_loop(0, NS - 1, greet_stream, 0)
    lax.fori_loop(0, NC - 1, greet_cross, 0)

    loads = []
    for i, (a, b) in enumerate(
        ((adj_h, adj), (up_h, up), (low_h, low), (src_h, src), (grad_h, grad), (ctrl_h, ctrl),
         (jac_h, jac), (left_h, left), (right_h, right))
    ):
        copy = pltpu.make_async_copy(a, b, in_sem.at[i])
        copy.start()
        loads.append(copy)

    def remote(a, b, n, where):
        return pltpu.make_async_remote_copy(
            src_ref=a, dst_ref=b, send_sem=send_sem.at[n], recv_sem=recv_sem.at[n],
            device_id=where, device_id_type=MESH,
        )

    def to_cross(n, source, dest):
        def body(k, carry):
            t = cross_peer(k)
            remote(source(t), dest.at[c], n, (s, t)).start()
            return carry

        lax.fori_loop(0, NC - 1, body, 0)

    sent = []
    after, before = (s + 1) % NS, (s + NS - 1) % NS

    def cell(ref, k, i):
        return ref[pl.ds(k * 160 + i, 40, stride=4), :]

    def pack(ref, k, four):
        for b, packed in enumerate(swap_blocks(four)):
            for f in range(NF):
                ref[pl.ds(b * 16 + k + f, 8, stride=64), :] = packed[f * 8 : f * 8 + 8]

    def mixed(matrix, array):
        parts = [array[g * 8 : g * 8 + 8] for g in range(NF)]
        rows = []
        for f in range(NF):
            value = matrix[f, 0] * parts[0]
            for g in range(1, NF):
                value += matrix[f, g] * parts[g]
            rows.append(value)
        return jnp.concatenate(rows, axis=0)

    loads[0].wait()
    own = [cell(adj, 0, i) for i in range(4)]
    loads[1].wait()
    diag = [cell(up, 0, i) for i in range(4)]
    next_s[0:40] = own[3]
    next_s[40:80] = diag[3]
    next_s[80:120] = diag[2]
    last_s[...] = own[0]
    inverse = [1.0 / d for d in diag]
    for k in (1, 2):
        pack(up_s, k * 5 - 5, [cell(up, k, i) * inverse[i] for i in range(4)])
    loads[2].wait()
    sub1 = [cell(low, 0, i) * inverse[i] for i in range(4)]
    sub2 = [cell(low, 1, i) * inverse[i] for i in range(4)]
    pack(
        up_s, 10, [sub1[1] * diag[0], sub1[2] * diag[1], sub1[3] * diag[2], sub2[2] * diag[0]]
    )

    for n in (3, 6, 7, 8):
        loads[n].wait()
    zero = jnp.zeros((40, 128), F32)
    line = [zero] + own + [zero]
    rhs = []
    for i in range(4):
        smooth = cell(src, 0, i) + dissipation * (line[i + 2] - 2.0 * line[i + 1] + line[i])
        residual = smooth - 0.5 * mixed(jac, line[i + 2] - line[i])
        rhs.append(mixed(left, residual) * inverse[i])

    pl.semaphore_wait(barrier, NS - 1 + NC - 1)
    behind_copies = [remote(next_s.at[pl.ds(i * 40, 40)], next_r.at[pl.ds(i * 40, 40)], (0, 8, 9)[i], (after, c)) for i in range(3)]
    ahead_copy = remote(last_s, last_r, 1, (before, c))
    behind_copies[0].start()
    ahead_copy.start()
    behind_copies[1].start()
    behind_copies[2].start()

    def to_owners(n, source, dest, rows):
        def body(k, carry):
            t = peer(k)
            remote(
                source.at[pl.ds(pl.multiple_of(t * 16, 16), rows)],
                dest.at[pl.ds(pl.multiple_of(s * 16, 16), rows)], n, (t, c),
            ).start()
            return carry

        lax.fori_loop(0, NS - 1, body, 0)
        mine = pl.ds(pl.multiple_of(s * 16, 16), 16)
        dest[mine, :] = source[mine, :]

    to_owners(2, up_s, up_r, 15)

    behind_copies[0].wait_recv()
    ahead_copy.wait_recv()
    first = jnp.where(s == 0, 0.0, next_r[0:40])
    last = jnp.where(s == NS - 1, 0.0, last_r[...])
    rhs[0] += mixed(left, 0.5 * mixed(jac, first) + dissipation * first) * inverse[0]
    rhs[3] += mixed(left, dissipation * last - 0.5 * mixed(jac, last)) * inverse[3]
    pack(low_s, 0, [sub2[3] * diag[1], rhs[1], rhs[2], rhs[0]])
    behind_copies[1].wait_recv()
    behind_copies[2].wait_recv()
    sent += [*behind_copies, ahead_copy]
    diag1, diag2 = next_r[40:80], next_r[80:120]
    pack(low_s, 5, [sub1[0] * diag1, sub2[0] * diag2, sub2[1] * diag1, rhs[3]])
    to_owners(3, low_s, low_r, 10)

    loads[4].wait()
    loads[5].wait()
    terms = adj[0:32] * grad[0:32]
    for f in range(1, NF):
        terms += adj[f * 32 : f * 32 + 32] * grad[f * 32 : f * 32 + 32]
    coarse = terms.astype(jnp.bfloat16).astype(F32)
    fine = terms - coarse
    where = ctrl[...]
    high_part, low_part = where // 128, where % 128
    rows = lax.broadcasted_iota(jnp.int32, (128, 128), 0)
    for r in range(32):
        at = slice(r * 128, r * 128 + 128)
        hot_a[:, at] = jnp.where(rows == high_part[r : r + 1], 1.0, 0.0).astype(jnp.bfloat16)
        hit = rows == low_part[r : r + 1]
        hot_b[0:128, at] = jnp.where(hit, coarse[r : r + 1], 0.0).astype(jnp.bfloat16)
        hot_b[128:256, at] = jnp.where(hit, fine[r : r + 1], 0.0).astype(jnp.bfloat16)
    both = lax.dot_general(
        hot_a[...], hot_b[...], (((1,), (1,)), ((), ())), preferred_element_type=F32
    )
    sums[...] = (both[:, 0:128] + both[:, 128:256]).reshape(16, 8, 128)
    to_cross(4, lambda t: sums.at[t], cross_r)
    cross_r[c] = sums[c]

    block = block_of((40, 128))

    def unpack(ref, k):
        per_x = [
            jnp.concatenate(
                [ref[pl.ds(x * 16 + k * 5 + f, 8, stride=64), :] for f in range(NF)], axis=0
            )
            for x in range(4)
        ]
        return swap_blocks(per_x)

    def moved(values, shift, edge, fill):
        return tuple(
            jnp.where(edge, value, pltpu.roll(entry, shift, 1)) for entry, value in zip(values, fill)
        )

    unit = (1.0, 0.0, 0.0, 1.0)
    none = (0.0, 0.0)

    def prefix_mats(mats, shifts, edges):
        one = mat_mul(mats, moved(mats, shifts[0], edges[0], unit))
        two = mat_mul(one, moved(one, shifts[1], edges[1], unit))
        return one, two, moved(two, shifts[0], edges[0], unit)

    def prefix_vecs(mats, one, vecs, shifts, edges):
        moved_vecs = mat_vec(mats, moved(vecs, shifts[0], edges[0], none))
        first_vecs = tuple(a + b for a, b in zip(moved_vecs, vecs))
        moved_vecs = mat_vec(one, moved(first_vecs, shifts[1], edges[1], none))
        second = tuple(a + b for a, b in zip(moved_vecs, first_vecs))
        return second, moved(second, shifts[0], edges[0], none)

    def walk(mats, vecs, order, keep):
        for n, entry in enumerate((*mats, *vecs)):
            maps[n] = entry
        state = (jnp.zeros((NF, 128), F32),) * 2
        for z in order:
            rows_z = pl.ds(z, NF, stride=8)
            states[0, rows_z, :] = state[0]
            states[1, rows_z, :] = state[1]
            if z != order[-1]:
                at_z = [maps[n, rows_z, :] for n in range(6)]
                state = tuple(a + b for a, b in zip(mat_vec(at_z[:4], state), at_z[4:]))
        spread = []
        for n in range(2):
            value = jnp.where(block == keep, states[n], 0.0)
            value = value + pltpu.roll(value, 64, 1)
            spread.append(value + pltpu.roll(value, 32, 1))
        return spread

    def entering(mats, vecs, state):
        return tuple(a + b for a, b in zip(mat_vec(mats, state), vecs))

    def arrived(n, a, b, count, where):
        copy = remote(a.at[pl.ds(0, count)], b.at[pl.ds(0, count)], n, where)
        copy.wait_recv()
        sent.append(copy)

    arrived(2, up_s, up_r, (NS - 1) * 15, (after, c))
    alpha, beta = unpack(up_r, 0), unpack(up_r, 1)
    sub1, sub2 = [None] * 4, [None] * 4
    sub1[1], sub1[2], sub1[3], sub2[2] = unpack(up_r, 2)
    bp, bq = [None] * 4, [None] * 4
    bp[3], bq[3] = -alpha[3], -beta[3]
    bp[2], bq[2] = -alpha[2] * bp[3] - beta[2], -alpha[2] * bq[3]
    for i in (1, 0):
        bp[i] = -alpha[i] * bp[i + 1] - beta[i] * bp[i + 2]
        bq[i] = -alpha[i] * bq[i + 1] - beta[i] * bq[i + 2]
    b_shifts, b_edges = (96, 64), (block == 3, block >= 2)
    b_mats = (bp[0], bq[0], bp[1], bq[1])
    b_one, b_two, b_before = prefix_mats(b_mats, b_shifts, b_edges)

    arrived(3, low_s, low_r, (NS - 1) * 10, (after, c))
    rhs = [None] * 4
    sub2[3], rhs[1], rhs[2], rhs[0] = unpack(low_r, 0)
    sub1[0], sub2[0], sub2[1], rhs[3] = unpack(low_r, 1)
    fp, fq, fr = [-sub1[0]], [-sub2[0]], [rhs[0]]
    fp.append(-sub1[1] * fp[0] - sub2[1])
    fq.append(-sub1[1] * fq[0])
    fr.append(rhs[1] - sub1[1] * fr[0])
    for i in (2, 3):
        fp.append(-sub1[i] * fp[i - 1] - sub2[i] * fp[i - 2])
        fq.append(-sub1[i] * fq[i - 1] - sub2[i] * fq[i - 2])
        fr.append(rhs[i] - sub1[i] * fr[i - 1] - sub2[i] * fr[i - 2])
    f_shifts, f_edges = (32, 64), (block == 0, block < 2)
    f_mats = (fp[3], fq[3], fp[2], fq[2])
    f_one, f_two, f_before = prefix_mats(f_mats, f_shifts, f_edges)
    f_vecs, f_vecs_before = prefix_vecs(f_mats, f_one, (fr[3], fr[2]), f_shifts, f_edges)
    state = walk(f_two, f_vecs, list(range(8)), 3)
    enter = entering(f_before, f_vecs_before, state)
    gamma = [fp[i] * enter[0] + fq[i] * enter[1] + fr[i] for i in range(4)]

    br = [None] * 4
    br[3] = gamma[3]
    br[2] = gamma[2] - alpha[2] * br[3]
    for i in (1, 0):
        br[i] = gamma[i] - alpha[i] * br[i + 1] - beta[i] * br[i + 2]
    b_vecs, b_vecs_before = prefix_vecs(b_mats, b_one, (br[0], br[1]), b_shifts, b_edges)
    state = walk(b_two, b_vecs, list(range(7, -1, -1)), 0)
    enter = entering(b_before, b_vecs_before, state)
    solved = [bp[i] * enter[0] + bq[i] * enter[1] + br[i] for i in range(4)]

    increment = [mixed(right, entry) for entry in solved]
    squares = sum(entry * entry for entry in increment)
    squares = sum(squares[f * 8 : f * 8 + 8] for f in range(NF))

    sq_s[...] = jnp.broadcast_to(jnp.sum(squares, axis=0, keepdims=True), (8, 128))
    one_row = pl.ds(0, 1)

    def body_sq(k, carry):
        t = cross_peer(k)
        remote(sq_s.at[one_row], sq_r.at[c, one_row], 5, (s, t)).start()
        return carry

    lax.fori_loop(0, NC - 1, body_sq, 0)
    sq_r[c] = sq_s[...]

    for x, packed in enumerate(swap_blocks(increment)):
        for f in range(NF):
            inc_s[pl.ds(x * 8 + f, 8, stride=32), :] = packed[f * 8 : f * 8 + 8]

    def body_inc(k, carry):
        t = peer(k)
        remote(
            inc_s.at[pl.ds(pl.multiple_of(t * 8, 8), 8)],
            inc_r.at[pl.ds(pl.multiple_of(s * 8, 8), 8)], 6, (t, c),
        ).start()
        return carry

    lax.fori_loop(0, NS - 1, body_inc, 0)
    eight = pl.ds(pl.multiple_of(s * 8, 8), 8)
    inc_r[eight, :] = inc_s[eight, :]

    def rows_arrived(n, ref, count, where):
        copy = remote(ref.at[pl.ds(0, count), 0], ref.at[pl.ds(0, count), 0], n, where)
        copy.wait_recv()
        sent.append(copy)

    rows_arrived(5, sq_r, NC - 1, (s, (c + 1) % NC))
    sq2_s[...] = jnp.broadcast_to(
        jnp.sum(sq_r[:, 0, :], axis=0, keepdims=True), (8, 128)
    )

    def body_sq2(k, carry):
        t = peer(k)
        remote(sq2_s.at[one_row], sq2_r.at[s, one_row], 7, (t, c)).start()
        return carry

    lax.fori_loop(0, NS - 1, body_sq2, 0)
    sq2_r[s] = sq2_s[...]

    arrived(4, sums, cross_r, NC - 1, (s, (c + 1) % NC))
    sens[...] = jnp.sum(cross_r[...], axis=0)

    arrived(6, inc_s, inc_r, (NS - 1) * 8, (after, c))
    per_b = [
        jnp.concatenate(
            [inc_r[pl.ds(b * 8 + f, 8, stride=32), :] for f in range(NF)], axis=0
        )
        for b in range(4)
    ]
    mine_inc = swap_blocks(per_b)

    rows_arrived(7, sq2_r, NS - 1, (after, c))
    total = jnp.sum(jnp.sum(sq2_r[:, 0, :], axis=0, keepdims=True), axis=1, keepdims=True)
    scale = step_scale / jnp.sqrt(total * (1.0 / CELLS) + epsilon)
    for i in range(4):
        out[pl.ds(i, 40, stride=4), :] = own[i] + mine_inc[i] * scale
    for copy in sent:
        copy.wait_send()


def rows_of(array):
    lead = array.shape[:-2]
    array = array.reshape(*lead, 4, 8, 128)
    return jnp.swapaxes(array, -3, -2).reshape(-1, 128)


def shards(adjoint, source, shape_grad, lower_band, upper_band, jacobian, left, right, ctrl_local):
    vmem = pltpu.VMEM
    hbm = pl.BlockSpec(memory_space=pl.ANY)
    out, sens = pl.pallas_call(
        kernel,
        out_shape=(jax.ShapeDtypeStruct((160, 128), F32), jax.ShapeDtypeStruct((8, 128), F32)),
        in_specs=[hbm] * 9,
        out_specs=(pl.BlockSpec(memory_space=vmem),) * 2,
        scratch_shapes=[
            pltpu.SMEM((NF, NF), F32),
            pltpu.SMEM((NF, NF), F32),
            pltpu.SMEM((NF, NF), F32),
            vmem((160, 128), F32),
            vmem((160, 128), F32),
            vmem((160, 128), F32),
            vmem((320, 128), F32),
            vmem((480, 128), F32),
            vmem((32, 128), jnp.int32),
            vmem((120, 128), F32),
            vmem((120, 128), F32),
            vmem((40, 128), F32),
            vmem((40, 128), F32),
            vmem((512, 128), F32),
            vmem((512, 128), F32),
            vmem((512, 128), F32),
            vmem((512, 128), F32),
            vmem((256, 128), F32),
            vmem((256, 128), F32),
            vmem((128, 4096), jnp.bfloat16),
            vmem((256, 4096), jnp.bfloat16),
            vmem((16, 8, 128), F32),
            vmem((16, 8, 128), F32),
            vmem((8, 128), F32),
            vmem((16, 8, 128), F32),
            vmem((8, 128), F32),
            vmem((32, 8, 128), F32),
            vmem((6, 40, 128), F32),
            vmem((2, 40, 128), F32),
            pltpu.SemaphoreType.DMA((9,)),
            pltpu.SemaphoreType.DMA((10,)),
            pltpu.SemaphoreType.DMA((10,)),
        ],
        compiler_params=pltpu.CompilerParams(
            collective_id=0, has_side_effects=True, vmem_limit_bytes=40 * 2**20
        ),
    )(
        *(pltpu.with_memory_space_constraint(x, pltpu.HBM) for x in (
        jacobian, left, right,
        rows_of(adjoint), rows_of(source), rows_of(shape_grad), rows_of(lower_band),
        rows_of(upper_band), rows_of(ctrl_local)))
    )
    adjoint_next = jnp.swapaxes(out.reshape(NF, 8, 4, 128), 1, 2).reshape(NF, 4, 1024)
    return adjoint_next, sens.reshape(1024)


def solution(mesh):
    cells = P(None, "stream", "cross")
    bands = P(None, None, "stream", "cross")
    in_specs = (cells, cells, cells, bands, bands, P(), P(), P(), P("stream", "cross"))
    out_specs = (cells, P(("stream", "cross")))
    return jax.shard_map(shards, mesh=mesh, in_specs=in_specs, out_specs=out_specs, check_vma=False)
```

```python
import jax
import jax.numpy as jnp
from jax import lax
from jax.experimental import pallas as pl
from jax.experimental.pallas import tpu as pltpu
from jax.sharding import PartitionSpec as P

MESH = pl.DeviceIdType.MESH
NF, CELLS = 5, 5 * 128 * 16384
NS, NC = 32, 16
dissipation = 0.25
step_scale = 0.5
epsilon = 1e-06
F32 = jnp.float32


def block_of(shape):
    return lax.broadcasted_iota(jnp.int32, shape, 1) // 32


def swap_blocks(four):
    block = block_of(four[0].shape)
    low, even = block < 2, block % 2 == 0
    a0, a1, a2, a3 = four
    m0 = pltpu.roll(jnp.where(low, a2, a0), 64, 1)
    m1 = pltpu.roll(jnp.where(low, a3, a1), 64, 1)
    x0, x2 = jnp.where(low, a0, m0), jnp.where(low, m0, a2)
    x1, x3 = jnp.where(low, a1, m1), jnp.where(low, m1, a3)
    return [
        jnp.where(even, x0, pltpu.roll(x1, 32, 1)),
        jnp.where(even, pltpu.roll(x0, 96, 1), x1),
        jnp.where(even, x2, pltpu.roll(x3, 32, 1)),
        jnp.where(even, pltpu.roll(x2, 96, 1), x3),
    ]


def mat_mul(a, b):
    return (
        a[0] * b[0] + a[1] * b[2],
        a[0] * b[1] + a[1] * b[3],
        a[2] * b[0] + a[3] * b[2],
        a[2] * b[1] + a[3] * b[3],
    )


def mat_vec(a, v):
    return (a[0] * v[0] + a[1] * v[1], a[2] * v[0] + a[3] * v[1])


def kernel(
    jac_h, left_h, right_h, adj_h, src_h, grad_h, low_h, up_h, ctrl_h,
    out, sens,
    jac, left, right, adj, src, grad, low, up, ctrl, next_s, next_r, last_s, last_r, up_s, up_r, low_s, low_r, inc_s, inc_r,
    hot_a, hot_b, sums, cross_r, sq_s, sq_r, sq2_s, sq2_r, maps, states,
    in_sem, send_sem, recv_sem,
):
    s, c = lax.axis_index("stream"), lax.axis_index("cross")

    def peer(k):
        m, n = k // 4, k % 4
        z = (s // 4 + 4 + (m + 1) // 2 * (1 - 2 * (m % 2))) % 8
        x = (s % 4 + 2 + (n + 1) // 2 * (1 - 2 * (n % 2))) % 4
        return z * 4 + x

    def cross_peer(k):
        m, n = k // 2, k % 2
        y = (c // 2 + 4 + (m + 1) // 2 * (1 - 2 * (m % 2))) % 8
        return y * 2 + (c + n + 1) % 2

    barrier = pltpu.get_barrier_semaphore()

    def greet_stream(k, carry):
        pl.semaphore_signal(barrier, inc=1, device_id=(peer(k), c), device_id_type=MESH)
        return carry

    def greet_cross(k, carry):
        pl.semaphore_signal(barrier, inc=1, device_id=(s, cross_peer(k)), device_id_type=MESH)
        return carry

    lax.fori_loop(0, NS - 1, greet_stream, 0)
    lax.fori_loop(0, NC - 1, greet_cross, 0)

    loads = []
    for i, (a, b) in enumerate(
        ((adj_h, adj), (up_h, up), (low_h, low), (src_h, src), (grad_h, grad), (ctrl_h, ctrl),
         (jac_h, jac), (left_h, left), (right_h, right))
    ):
        copy = pltpu.make_async_copy(a, b, in_sem.at[i])
        copy.start()
        loads.append(copy)

    def remote(a, b, n, where):
        return pltpu.make_async_remote_copy(
            src_ref=a, dst_ref=b, send_sem=send_sem.at[n], recv_sem=recv_sem.at[n],
            device_id=where, device_id_type=MESH,
        )

    def to_cross(n, source, dest):
        def body(k, carry):
            t = cross_peer(k)
            remote(source(t), dest.at[c], n, (s, t)).start()
            return carry

        lax.fori_loop(0, NC - 1, body, 0)

    sent = []
    after, before = (s + 1) % NS, (s + NS - 1) % NS

    def cell(ref, k, i):
        return ref[pl.ds(k * 160 + i, 40, stride=4), :]

    def pack(ref, k, four):
        for b, packed in enumerate(swap_blocks(four)):
            for f in range(NF):
                ref[pl.ds(b * 16 + k + f, 8, stride=64), :] = packed[f * 8 : f * 8 + 8]

    def mixed(matrix, array):
        parts = [array[g * 8 : g * 8 + 8] for g in range(NF)]
        rows = []
        for f in range(NF):
            value = matrix[f, 0] * parts[0]
            for g in range(1, NF):
                value += matrix[f, g] * parts[g]
            rows.append(value)
        return jnp.concatenate(rows, axis=0)

    loads[0].wait()
    own = [cell(adj, 0, i) for i in range(4)]
    loads[1].wait()
    diag = [cell(up, 0, i) for i in range(4)]
    next_s[0:40] = own[3]
    next_s[40:80] = diag[3]
    next_s[80:120] = diag[2]
    last_s[...] = own[0]
    inverse = [1.0 / d for d in diag]
    for k in (1, 2):
        pack(up_s, k * 5 - 5, [cell(up, k, i) * inverse[i] for i in range(4)])
    loads[2].wait()
    sub1 = [cell(low, 0, i) * inverse[i] for i in range(4)]
    sub2 = [cell(low, 1, i) * inverse[i] for i in range(4)]
    pack(
        up_s, 10, [sub1[1] * diag[0], sub1[2] * diag[1], sub1[3] * diag[2], sub2[2] * diag[0]]
    )

    for n in (3, 6, 7, 8):
        loads[n].wait()
    zero = jnp.zeros((40, 128), F32)
    line = [zero] + own + [zero]
    rhs = []
    for i in range(4):
        smooth = cell(src, 0, i) + dissipation * (line[i + 2] - 2.0 * line[i + 1] + line[i])
        residual = smooth - 0.5 * mixed(jac, line[i + 2] - line[i])
        rhs.append(mixed(left, residual) * inverse[i])

    pl.semaphore_wait(barrier, NS - 1 + NC - 1)
    behind_copies = [remote(next_s.at[pl.ds(i * 40, 40)], next_r.at[pl.ds(i * 40, 40)], (0, 8, 9)[i], (after, c)) for i in range(3)]
    ahead_copy = remote(last_s, last_r, 1, (before, c))
    behind_copies[0].start()
    ahead_copy.start()
    behind_copies[1].start()
    behind_copies[2].start()

    def to_owners(n, source, dest, rows):
        def body(k, carry):
            t = peer(k)
            remote(
                source.at[pl.ds(pl.multiple_of(t * 16, 16), rows)],
                dest.at[pl.ds(pl.multiple_of(s * 16, 16), rows)], n, (t, c),
            ).start()
            return carry

        lax.fori_loop(0, NS - 1, body, 0)
        mine = pl.ds(pl.multiple_of(s * 16, 16), 16)
        dest[mine, :] = source[mine, :]

    to_owners(2, up_s, up_r, 15)

    behind_copies[0].wait_recv()
    ahead_copy.wait_recv()
    first = jnp.where(s == 0, 0.0, next_r[0:40])
    last = jnp.where(s == NS - 1, 0.0, last_r[...])
    rhs[0] += mixed(left, 0.5 * mixed(jac, first) + dissipation * first) * inverse[0]
    rhs[3] += mixed(left, dissipation * last - 0.5 * mixed(jac, last)) * inverse[3]
    pack(low_s, 0, [sub2[3] * diag[1], rhs[1], rhs[2], rhs[0]])
    behind_copies[1].wait_recv()
    behind_copies[2].wait_recv()
    sent += [*behind_copies, ahead_copy]
    diag1, diag2 = next_r[40:80], next_r[80:120]
    pack(low_s, 5, [sub1[0] * diag1, sub2[0] * diag2, sub2[1] * diag1, rhs[3]])
    to_owners(3, low_s, low_r, 10)

    loads[4].wait()
    loads[5].wait()
    terms = adj[0:32] * grad[0:32]
    for f in range(1, NF):
        terms += adj[f * 32 : f * 32 + 32] * grad[f * 32 : f * 32 + 32]
    coarse = terms.astype(jnp.bfloat16).astype(F32)
    fine = terms - coarse
    where = ctrl[...]
    high_part, low_part = where // 128, where % 128
    rows = lax.broadcasted_iota(jnp.int32, (128, 128), 0)
    for r in range(32):
        at = slice(r * 128, r * 128 + 128)
        hot_a[:, at] = jnp.where(rows == high_part[r : r + 1], 1.0, 0.0).astype(jnp.bfloat16)
        hit = rows == low_part[r : r + 1]
        hot_b[0:128, at] = jnp.where(hit, coarse[r : r + 1], 0.0).astype(jnp.bfloat16)
        hot_b[128:256, at] = jnp.where(hit, fine[r : r + 1], 0.0).astype(jnp.bfloat16)
    both = lax.dot_general(
        hot_a[...], hot_b[...], (((1,), (1,)), ((), ())), preferred_element_type=F32
    )
    sums[...] = (both[:, 0:128] + both[:, 128:256]).reshape(16, 8, 128)
    to_cross(4, lambda t: sums.at[t], cross_r)
    cross_r[c] = sums[c]

    block = block_of((40, 128))

    def unpack(ref, k):
        per_x = [
            jnp.concatenate(
                [ref[pl.ds(x * 16 + k * 5 + f, 8, stride=64), :] for f in range(NF)], axis=0
            )
            for x in range(4)
        ]
        return swap_blocks(per_x)

    def moved(values, shift, edge, fill):
        return tuple(
            jnp.where(edge, value, pltpu.roll(entry, shift, 1)) for entry, value in zip(values, fill)
        )

    unit = (1.0, 0.0, 0.0, 1.0)
    none = (0.0, 0.0)

    def prefix_mats(mats, shifts, edges):
        one = mat_mul(mats, moved(mats, shifts[0], edges[0], unit))
        two = mat_mul(one, moved(one, shifts[1], edges[1], unit))
        return one, two, moved(two, shifts[0], edges[0], unit)

    def prefix_vecs(mats, one, vecs, shifts, edges):
        moved_vecs = mat_vec(mats, moved(vecs, shifts[0], edges[0], none))
        first_vecs = tuple(a + b for a, b in zip(moved_vecs, vecs))
        moved_vecs = mat_vec(one, moved(first_vecs, shifts[1], edges[1], none))
        second = tuple(a + b for a, b in zip(moved_vecs, first_vecs))
        return second, moved(second, shifts[0], edges[0], none)

    def walk(mats, vecs, order, keep):
        for n, entry in enumerate((*mats, *vecs)):
            maps[n] = entry
        state = (jnp.zeros((NF, 128), F32),) * 2
        for z in order:
            rows_z = pl.ds(z, NF, stride=8)
            states[0, rows_z, :] = state[0]
            states[1, rows_z, :] = state[1]
            if z != order[-1]:
                at_z = [maps[n, rows_z, :] for n in range(6)]
                state = tuple(a + b for a, b in zip(mat_vec(at_z[:4], state), at_z[4:]))
        spread = []
        for n in range(2):
            value = jnp.where(block == keep, states[n], 0.0)
            value = value + pltpu.roll(value, 64, 1)
            spread.append(value + pltpu.roll(value, 32, 1))
        return spread

    def entering(mats, vecs, state):
        return tuple(a + b for a, b in zip(mat_vec(mats, state), vecs))

    def arrived(n, a, b, count, where):
        copy = remote(a.at[pl.ds(0, count)], b.at[pl.ds(0, count)], n, where)
        copy.wait_recv()
        sent.append(copy)

    arrived(2, up_s, up_r, (NS - 1) * 15, (after, c))
    alpha, beta = unpack(up_r, 0), unpack(up_r, 1)
    sub1, sub2 = [None] * 4, [None] * 4
    sub1[1], sub1[2], sub1[3], sub2[2] = unpack(up_r, 2)
    bp, bq = [None] * 4, [None] * 4
    bp[3], bq[3] = -alpha[3], -beta[3]
    bp[2], bq[2] = -alpha[2] * bp[3] - beta[2], -alpha[2] * bq[3]
    for i in (1, 0):
        bp[i] = -alpha[i] * bp[i + 1] - beta[i] * bp[i + 2]
        bq[i] = -alpha[i] * bq[i + 1] - beta[i] * bq[i + 2]
    b_shifts, b_edges = (96, 64), (block == 3, block >= 2)
    b_mats = (bp[0], bq[0], bp[1], bq[1])
    b_one, b_two, b_before = prefix_mats(b_mats, b_shifts, b_edges)

    arrived(3, low_s, low_r, (NS - 1) * 10, (after, c))
    rhs = [None] * 4
    sub2[3], rhs[1], rhs[2], rhs[0] = unpack(low_r, 0)
    sub1[0], sub2[0], sub2[1], rhs[3] = unpack(low_r, 1)
    fp, fq, fr = [-sub1[0]], [-sub2[0]], [rhs[0]]
    fp.append(-sub1[1] * fp[0] - sub2[1])
    fq.append(-sub1[1] * fq[0])
    fr.append(rhs[1] - sub1[1] * fr[0])
    for i in (2, 3):
        fp.append(-sub1[i] * fp[i - 1] - sub2[i] * fp[i - 2])
        fq.append(-sub1[i] * fq[i - 1] - sub2[i] * fq[i - 2])
        fr.append(rhs[i] - sub1[i] * fr[i - 1] - sub2[i] * fr[i - 2])
    f_shifts, f_edges = (32, 64), (block == 0, block < 2)
    f_mats = (fp[3], fq[3], fp[2], fq[2])
    f_one, f_two, f_before = prefix_mats(f_mats, f_shifts, f_edges)
    f_vecs, f_vecs_before = prefix_vecs(f_mats, f_one, (fr[3], fr[2]), f_shifts, f_edges)
    state = walk(f_two, f_vecs, list(range(8)), 3)
    enter = entering(f_before, f_vecs_before, state)
    gamma = [fp[i] * enter[0] + fq[i] * enter[1] + fr[i] for i in range(4)]

    br = [None] * 4
    br[3] = gamma[3]
    br[2] = gamma[2] - alpha[2] * br[3]
    for i in (1, 0):
        br[i] = gamma[i] - alpha[i] * br[i + 1] - beta[i] * br[i + 2]
    b_vecs, b_vecs_before = prefix_vecs(b_mats, b_one, (br[0], br[1]), b_shifts, b_edges)
    state = walk(b_two, b_vecs, list(range(7, -1, -1)), 0)
    enter = entering(b_before, b_vecs_before, state)
    solved = [bp[i] * enter[0] + bq[i] * enter[1] + br[i] for i in range(4)]

    increment = [mixed(right, entry) for entry in solved]
    squares = sum(entry * entry for entry in increment)
    squares = sum(squares[f * 8 : f * 8 + 8] for f in range(NF))

    sq_s[...] = jnp.broadcast_to(jnp.sum(squares, axis=0, keepdims=True), (8, 128))
    one_row = pl.ds(0, 1)

    def body_sq(k, carry):
        t = cross_peer(k)
        remote(sq_s.at[one_row], sq_r.at[c, one_row], 5, (s, t)).start()
        return carry

    lax.fori_loop(0, NC - 1, body_sq, 0)
    sq_r[c] = sq_s[...]

    for x, packed in enumerate(swap_blocks(increment)):
        for f in range(NF):
            inc_s[pl.ds(x * 8 + f, 8, stride=32), :] = packed[f * 8 : f * 8 + 8]

    def body_inc(k, carry):
        t = peer(k)
        remote(
            inc_s.at[pl.ds(pl.multiple_of(t * 8, 8), NF)],
            inc_r.at[pl.ds(pl.multiple_of(s * 8, 8), NF)], 6, (t, c),
        ).start()
        return carry

    lax.fori_loop(0, NS - 1, body_inc, 0)
    eight = pl.ds(pl.multiple_of(s * 8, 8), 8)
    inc_r[eight, :] = inc_s[eight, :]

    def rows_arrived(n, ref, count, where):
        copy = remote(ref.at[pl.ds(0, count), 0], ref.at[pl.ds(0, count), 0], n, where)
        copy.wait_recv()
        sent.append(copy)

    rows_arrived(5, sq_r, NC - 1, (s, (c + 1) % NC))
    sq2_s[...] = jnp.broadcast_to(
        jnp.sum(sq_r[:, 0, :], axis=0, keepdims=True), (8, 128)
    )

    def body_sq2(k, carry):
        t = peer(k)
        remote(sq2_s.at[one_row], sq2_r.at[s, one_row], 7, (t, c)).start()
        return carry

    lax.fori_loop(0, NS - 1, body_sq2, 0)
    sq2_r[s] = sq2_s[...]

    arrived(4, sums, cross_r, NC - 1, (s, (c + 1) % NC))
    sens[...] = jnp.sum(cross_r[...], axis=0)

    arrived(6, inc_s, inc_r, (NS - 1) * NF, (after, c))
    per_b = [
        jnp.concatenate(
            [inc_r[pl.ds(b * 8 + f, 8, stride=32), :] for f in range(NF)], axis=0
        )
        for b in range(4)
    ]
    mine_inc = swap_blocks(per_b)

    rows_arrived(7, sq2_r, NS - 1, (after, c))
    total = jnp.sum(jnp.sum(sq2_r[:, 0, :], axis=0, keepdims=True), axis=1, keepdims=True)
    scale = step_scale / jnp.sqrt(total * (1.0 / CELLS) + epsilon)
    for i in range(4):
        out[pl.ds(i, 40, stride=4), :] = own[i] + mine_inc[i] * scale
    for copy in sent:
        copy.wait_send()


def rows_of(array):
    lead = array.shape[:-2]
    array = array.reshape(*lead, 4, 8, 128)
    return jnp.swapaxes(array, -3, -2).reshape(-1, 128)


def shards(adjoint, source, shape_grad, lower_band, upper_band, jacobian, left, right, ctrl_local):
    vmem = pltpu.VMEM
    hbm = pl.BlockSpec(memory_space=pl.ANY)
    out, sens = pl.pallas_call(
        kernel,
        out_shape=(jax.ShapeDtypeStruct((160, 128), F32), jax.ShapeDtypeStruct((8, 128), F32)),
        in_specs=[hbm] * 9,
        out_specs=(pl.BlockSpec(memory_space=vmem),) * 2,
        scratch_shapes=[
            pltpu.SMEM((NF, NF), F32),
            pltpu.SMEM((NF, NF), F32),
            pltpu.SMEM((NF, NF), F32),
            vmem((160, 128), F32),
            vmem((160, 128), F32),
            vmem((160, 128), F32),
            vmem((320, 128), F32),
            vmem((480, 128), F32),
            vmem((32, 128), jnp.int32),
            vmem((120, 128), F32),
            vmem((120, 128), F32),
            vmem((40, 128), F32),
            vmem((40, 128), F32),
            vmem((512, 128), F32),
            vmem((512, 128), F32),
            vmem((512, 128), F32),
            vmem((512, 128), F32),
            vmem((256, 128), F32),
            vmem((256, 128), F32),
            vmem((128, 4096), jnp.bfloat16),
            vmem((256, 4096), jnp.bfloat16),
            vmem((16, 8, 128), F32),
            vmem((16, 8, 128), F32),
            vmem((8, 128), F32),
            vmem((16, 8, 128), F32),
            vmem((8, 128), F32),
            vmem((32, 8, 128), F32),
            vmem((6, 40, 128), F32),
            vmem((2, 40, 128), F32),
            pltpu.SemaphoreType.DMA((9,)),
            pltpu.SemaphoreType.DMA((10,)),
            pltpu.SemaphoreType.DMA((10,)),
        ],
        compiler_params=pltpu.CompilerParams(
            collective_id=0, has_side_effects=True, vmem_limit_bytes=40 * 2**20
        ),
    )(
        *(pltpu.with_memory_space_constraint(x, pltpu.HBM) for x in (
        jacobian, left, right,
        rows_of(adjoint), rows_of(source), rows_of(shape_grad), rows_of(lower_band),
        rows_of(upper_band), rows_of(ctrl_local)))
    )
    adjoint_next = jnp.swapaxes(out.reshape(NF, 8, 4, 128), 1, 2).reshape(NF, 4, 1024)
    return adjoint_next, sens.reshape(1024)


def solution(mesh):
    cells = P(None, "stream", "cross")
    bands = P(None, None, "stream", "cross")
    in_specs = (cells, cells, cells, bands, bands, P(), P(), P(), P("stream", "cross"))
    out_specs = (cells, P(("stream", "cross")))
    return jax.shard_map(shards, mesh=mesh, in_specs=in_specs, out_specs=out_specs, check_vma=False)
```

```python
import jax
import jax.numpy as jnp
from jax import lax
from jax.experimental import pallas as pl
from jax.experimental.pallas import tpu as pltpu
from jax.sharding import PartitionSpec as P

MESH = pl.DeviceIdType.MESH
NF, CELLS = 5, 5 * 128 * 16384
NS, NC = 32, 16
dissipation = 0.25
step_scale = 0.5
epsilon = 1e-06
F32 = jnp.float32


def block_of(shape):
    return lax.broadcasted_iota(jnp.int32, shape, 1) // 32


def swap_blocks(four):
    block = block_of(four[0].shape)
    low, even = block < 2, block % 2 == 0
    a0, a1, a2, a3 = four
    m0 = pltpu.roll(jnp.where(low, a2, a0), 64, 1)
    m1 = pltpu.roll(jnp.where(low, a3, a1), 64, 1)
    x0, x2 = jnp.where(low, a0, m0), jnp.where(low, m0, a2)
    x1, x3 = jnp.where(low, a1, m1), jnp.where(low, m1, a3)
    return [
        jnp.where(even, x0, pltpu.roll(x1, 32, 1)),
        jnp.where(even, pltpu.roll(x0, 96, 1), x1),
        jnp.where(even, x2, pltpu.roll(x3, 32, 1)),
        jnp.where(even, pltpu.roll(x2, 96, 1), x3),
    ]


def mat_mul(a, b):
    return (
        a[0] * b[0] + a[1] * b[2],
        a[0] * b[1] + a[1] * b[3],
        a[2] * b[0] + a[3] * b[2],
        a[2] * b[1] + a[3] * b[3],
    )


def mat_vec(a, v):
    return (a[0] * v[0] + a[1] * v[1], a[2] * v[0] + a[3] * v[1])


def kernel(
    jac_h, left_h, right_h, adj_h, src_h, grad_h, low_h, up_h, ctrl_h,
    out, sens,
    jac, left, right, adj, src, grad, low, up, ctrl, next_s, next_r, last_s, last_r, up_s, up_r, low_s, low_r, inc_s, inc_r,
    hot_a, hot_b, sums, cross_r, sq_s, sq_r, sq2_s, sq2_r, maps, states,
    in_sem, send_sem, recv_sem,
):
    s, c = lax.axis_index("stream"), lax.axis_index("cross")

    def peer(k):
        m, n = k % 8, k // 8
        z = (s // 4 + 4 + (m + 1) // 2 * (1 - 2 * (m % 2))) % 8
        x = (s % 4 + 2 + (n + 1) // 2 * (1 - 2 * (n % 2))) % 4
        return z * 4 + x

    def cross_peer(k):
        m, n = k // 2, k % 2
        y = (c // 2 + 4 + (m + 1) // 2 * (1 - 2 * (m % 2))) % 8
        return y * 2 + (c + n + 1) % 2

    barrier = pltpu.get_barrier_semaphore()

    def greet_stream(k, carry):
        pl.semaphore_signal(barrier, inc=1, device_id=(peer(k), c), device_id_type=MESH)
        return carry

    def greet_cross(k, carry):
        pl.semaphore_signal(barrier, inc=1, device_id=(s, cross_peer(k)), device_id_type=MESH)
        return carry

    lax.fori_loop(0, NS - 1, greet_stream, 0)
    lax.fori_loop(0, NC - 1, greet_cross, 0)

    loads = []
    for i, (a, b) in enumerate(
        ((adj_h, adj), (up_h, up), (low_h, low), (src_h, src), (grad_h, grad), (ctrl_h, ctrl),
         (jac_h, jac), (left_h, left), (right_h, right))
    ):
        copy = pltpu.make_async_copy(a, b, in_sem.at[i])
        copy.start()
        loads.append(copy)

    def remote(a, b, n, where):
        return pltpu.make_async_remote_copy(
            src_ref=a, dst_ref=b, send_sem=send_sem.at[n], recv_sem=recv_sem.at[n],
            device_id=where, device_id_type=MESH,
        )

    def to_cross(n, source, dest):
        def body(k, carry):
            t = cross_peer(k)
            remote(source(t), dest.at[c], n, (s, t)).start()
            return carry

        lax.fori_loop(0, NC - 1, body, 0)

    sent = []
    after, before = (s + 1) % NS, (s + NS - 1) % NS

    def cell(ref, k, i):
        return ref[pl.ds(k * 160 + i, 40, stride=4), :]

    def pack(ref, k, four):
        for b, packed in enumerate(swap_blocks(four)):
            for f in range(NF):
                ref[pl.ds(b * 16 + k + f, 8, stride=64), :] = packed[f * 8 : f * 8 + 8]

    def mixed(matrix, array):
        parts = [array[g * 8 : g * 8 + 8] for g in range(NF)]
        rows = []
        for f in range(NF):
            value = matrix[f, 0] * parts[0]
            for g in range(1, NF):
                value += matrix[f, g] * parts[g]
            rows.append(value)
        return jnp.concatenate(rows, axis=0)

    loads[0].wait()
    own = [cell(adj, 0, i) for i in range(4)]
    loads[1].wait()
    diag = [cell(up, 0, i) for i in range(4)]
    next_s[0:40] = own[3]
    next_s[40:80] = diag[3]
    next_s[80:120] = diag[2]
    last_s[...] = own[0]
    inverse = [1.0 / d for d in diag]
    for k in (1, 2):
        pack(up_s, k * 5 - 5, [cell(up, k, i) * inverse[i] for i in range(4)])
    loads[2].wait()
    sub1 = [cell(low, 0, i) * inverse[i] for i in range(4)]
    sub2 = [cell(low, 1, i) * inverse[i] for i in range(4)]
    pack(
        up_s, 10, [sub1[1] * diag[0], sub1[2] * diag[1], sub1[3] * diag[2], sub2[2] * diag[0]]
    )

    for n in (3, 6, 7, 8):
        loads[n].wait()
    zero = jnp.zeros((40, 128), F32)
    line = [zero] + own + [zero]
    rhs = []
    for i in range(4):
        smooth = cell(src, 0, i) + dissipation * (line[i + 2] - 2.0 * line[i + 1] + line[i])
        residual = smooth - 0.5 * mixed(jac, line[i + 2] - line[i])
        rhs.append(mixed(left, residual) * inverse[i])

    pl.semaphore_wait(barrier, NS - 1 + NC - 1)
    behind_copies = [remote(next_s.at[pl.ds(i * 40, 40)], next_r.at[pl.ds(i * 40, 40)], (0, 8, 9)[i], (after, c)) for i in range(3)]
    ahead_copy = remote(last_s, last_r, 1, (before, c))
    behind_copies[0].start()
    ahead_copy.start()
    behind_copies[1].start()
    behind_copies[2].start()

    def to_owners(n, source, dest, rows):
        def body(k, carry):
            t = peer(k)
            remote(
                source.at[pl.ds(pl.multiple_of(t * 16, 16), rows)],
                dest.at[pl.ds(pl.multiple_of(s * 16, 16), rows)], n, (t, c),
            ).start()
            return carry

        lax.fori_loop(0, NS - 1, body, 0)
        mine = pl.ds(pl.multiple_of(s * 16, 16), 16)
        dest[mine, :] = source[mine, :]

    to_owners(2, up_s, up_r, 15)

    behind_copies[0].wait_recv()
    ahead_copy.wait_recv()
    first = jnp.where(s == 0, 0.0, next_r[0:40])
    last = jnp.where(s == NS - 1, 0.0, last_r[...])
    rhs[0] += mixed(left, 0.5 * mixed(jac, first) + dissipation * first) * inverse[0]
    rhs[3] += mixed(left, dissipation * last - 0.5 * mixed(jac, last)) * inverse[3]
    pack(low_s, 0, [sub2[3] * diag[1], rhs[1], rhs[2], rhs[0]])
    behind_copies[1].wait_recv()
    behind_copies[2].wait_recv()
    sent += [*behind_copies, ahead_copy]
    diag1, diag2 = next_r[40:80], next_r[80:120]
    pack(low_s, 5, [sub1[0] * diag1, sub2[0] * diag2, sub2[1] * diag1, rhs[3]])
    to_owners(3, low_s, low_r, 10)

    loads[4].wait()
    loads[5].wait()
    terms = adj[0:32] * grad[0:32]
    for f in range(1, NF):
        terms += adj[f * 32 : f * 32 + 32] * grad[f * 32 : f * 32 + 32]
    coarse = terms.astype(jnp.bfloat16).astype(F32)
    fine = terms - coarse
    where = ctrl[...]
    high_part, low_part = where // 128, where % 128
    rows = lax.broadcasted_iota(jnp.int32, (128, 128), 0)
    for r in range(32):
        at = slice(r * 128, r * 128 + 128)
        hot_a[:, at] = jnp.where(rows == high_part[r : r + 1], 1.0, 0.0).astype(jnp.bfloat16)
        hit = rows == low_part[r : r + 1]
        hot_b[0:128, at] = jnp.where(hit, coarse[r : r + 1], 0.0).astype(jnp.bfloat16)
        hot_b[128:256, at] = jnp.where(hit, fine[r : r + 1], 0.0).astype(jnp.bfloat16)
    both = lax.dot_general(
        hot_a[...], hot_b[...], (((1,), (1,)), ((), ())), preferred_element_type=F32
    )
    sums[...] = (both[:, 0:128] + both[:, 128:256]).reshape(16, 8, 128)
    to_cross(4, lambda t: sums.at[t], cross_r)
    cross_r[c] = sums[c]

    block = block_of((40, 128))

    def unpack(ref, k):
        per_x = [
            jnp.concatenate(
                [ref[pl.ds(x * 16 + k * 5 + f, 8, stride=64), :] for f in range(NF)], axis=0
            )
            for x in range(4)
        ]
        return swap_blocks(per_x)

    def moved(values, shift, edge, fill):
        return tuple(
            jnp.where(edge, value, pltpu.roll(entry, shift, 1)) for entry, value in zip(values, fill)
        )

    unit = (1.0, 0.0, 0.0, 1.0)
    none = (0.0, 0.0)

    def prefix_mats(mats, shifts, edges):
        one = mat_mul(mats, moved(mats, shifts[0], edges[0], unit))
        two = mat_mul(one, moved(one, shifts[1], edges[1], unit))
        return one, two, moved(two, shifts[0], edges[0], unit)

    def prefix_vecs(mats, one, vecs, shifts, edges):
        moved_vecs = mat_vec(mats, moved(vecs, shifts[0], edges[0], none))
        first_vecs = tuple(a + b for a, b in zip(moved_vecs, vecs))
        moved_vecs = mat_vec(one, moved(first_vecs, shifts[1], edges[1], none))
        second = tuple(a + b for a, b in zip(moved_vecs, first_vecs))
        return second, moved(second, shifts[0], edges[0], none)

    def walk(mats, vecs, order, keep):
        for n, entry in enumerate((*mats, *vecs)):
            maps[n] = entry
        state = (jnp.zeros((NF, 128), F32),) * 2
        for z in order:
            rows_z = pl.ds(z, NF, stride=8)
            states[0, rows_z, :] = state[0]
            states[1, rows_z, :] = state[1]
            if z != order[-1]:
                at_z = [maps[n, rows_z, :] for n in range(6)]
                state = tuple(a + b for a, b in zip(mat_vec(at_z[:4], state), at_z[4:]))
        spread = []
        for n in range(2):
            value = jnp.where(block == keep, states[n], 0.0)
            value = value + pltpu.roll(value, 64, 1)
            spread.append(value + pltpu.roll(value, 32, 1))
        return spread

    def entering(mats, vecs, state):
        return tuple(a + b for a, b in zip(mat_vec(mats, state), vecs))

    def arrived(n, a, b, count, where):
        copy = remote(a.at[pl.ds(0, count)], b.at[pl.ds(0, count)], n, where)
        copy.wait_recv()
        sent.append(copy)

    arrived(2, up_s, up_r, (NS - 1) * 15, (after, c))
    alpha, beta = unpack(up_r, 0), unpack(up_r, 1)
    sub1, sub2 = [None] * 4, [None] * 4
    sub1[1], sub1[2], sub1[3], sub2[2] = unpack(up_r, 2)
    bp, bq = [None] * 4, [None] * 4
    bp[3], bq[3] = -alpha[3], -beta[3]
    bp[2], bq[2] = -alpha[2] * bp[3] - beta[2], -alpha[2] * bq[3]
    for i in (1, 0):
        bp[i] = -alpha[i] * bp[i + 1] - beta[i] * bp[i + 2]
        bq[i] = -alpha[i] * bq[i + 1] - beta[i] * bq[i + 2]
    b_shifts, b_edges = (96, 64), (block == 3, block >= 2)
    b_mats = (bp[0], bq[0], bp[1], bq[1])
    b_one, b_two, b_before = prefix_mats(b_mats, b_shifts, b_edges)

    arrived(3, low_s, low_r, (NS - 1) * 10, (after, c))
    rhs = [None] * 4
    sub2[3], rhs[1], rhs[2], rhs[0] = unpack(low_r, 0)
    sub1[0], sub2[0], sub2[1], rhs[3] = unpack(low_r, 1)
    fp, fq, fr = [-sub1[0]], [-sub2[0]], [rhs[0]]
    fp.append(-sub1[1] * fp[0] - sub2[1])
    fq.append(-sub1[1] * fq[0])
    fr.append(rhs[1] - sub1[1] * fr[0])
    for i in (2, 3):
        fp.append(-sub1[i] * fp[i - 1] - sub2[i] * fp[i - 2])
        fq.append(-sub1[i] * fq[i - 1] - sub2[i] * fq[i - 2])
        fr.append(rhs[i] - sub1[i] * fr[i - 1] - sub2[i] * fr[i - 2])
    f_shifts, f_edges = (32, 64), (block == 0, block < 2)
    f_mats = (fp[3], fq[3], fp[2], fq[2])
    f_one, f_two, f_before = prefix_mats(f_mats, f_shifts, f_edges)
    f_vecs, f_vecs_before = prefix_vecs(f_mats, f_one, (fr[3], fr[2]), f_shifts, f_edges)
    state = walk(f_two, f_vecs, list(range(8)), 3)
    enter = entering(f_before, f_vecs_before, state)
    gamma = [fp[i] * enter[0] + fq[i] * enter[1] + fr[i] for i in range(4)]

    br = [None] * 4
    br[3] = gamma[3]
    br[2] = gamma[2] - alpha[2] * br[3]
    for i in (1, 0):
        br[i] = gamma[i] - alpha[i] * br[i + 1] - beta[i] * br[i + 2]
    b_vecs, b_vecs_before = prefix_vecs(b_mats, b_one, (br[0], br[1]), b_shifts, b_edges)
    state = walk(b_two, b_vecs, list(range(7, -1, -1)), 0)
    enter = entering(b_before, b_vecs_before, state)
    solved = [bp[i] * enter[0] + bq[i] * enter[1] + br[i] for i in range(4)]

    increment = [mixed(right, entry) for entry in solved]
    squares = sum(entry * entry for entry in increment)
    squares = sum(squares[f * 8 : f * 8 + 8] for f in range(NF))

    sq_s[...] = jnp.broadcast_to(jnp.sum(squares, axis=0, keepdims=True), (8, 128))
    one_row = pl.ds(0, 1)

    def body_sq(k, carry):
        t = cross_peer(k)
        remote(sq_s.at[one_row], sq_r.at[c, one_row], 5, (s, t)).start()
        return carry

    lax.fori_loop(0, NC - 1, body_sq, 0)
    sq_r[c] = sq_s[...]

    for x, packed in enumerate(swap_blocks(increment)):
        for f in range(NF):
            inc_s[pl.ds(x * 8 + f, 8, stride=32), :] = packed[f * 8 : f * 8 + 8]

    def body_inc(k, carry):
        t = peer(k)
        remote(
            inc_s.at[pl.ds(pl.multiple_of(t * 8, 8), NF)],
            inc_r.at[pl.ds(pl.multiple_of(s * 8, 8), NF)], 6, (t, c),
        ).start()
        return carry

    lax.fori_loop(0, NS - 1, body_inc, 0)
    eight = pl.ds(pl.multiple_of(s * 8, 8), 8)
    inc_r[eight, :] = inc_s[eight, :]

    def rows_arrived(n, ref, count, where):
        copy = remote(ref.at[pl.ds(0, count), 0], ref.at[pl.ds(0, count), 0], n, where)
        copy.wait_recv()
        sent.append(copy)

    rows_arrived(5, sq_r, NC - 1, (s, (c + 1) % NC))
    sq2_s[...] = jnp.broadcast_to(
        jnp.sum(sq_r[:, 0, :], axis=0, keepdims=True), (8, 128)
    )

    def body_sq2(k, carry):
        t = peer(k)
        remote(sq2_s.at[one_row], sq2_r.at[s, one_row], 7, (t, c)).start()
        return carry

    lax.fori_loop(0, NS - 1, body_sq2, 0)
    sq2_r[s] = sq2_s[...]

    arrived(4, sums, cross_r, NC - 1, (s, (c + 1) % NC))
    sens[...] = jnp.sum(cross_r[...], axis=0)

    arrived(6, inc_s, inc_r, (NS - 1) * NF, (after, c))
    per_b = [
        jnp.concatenate(
            [inc_r[pl.ds(b * 8 + f, 8, stride=32), :] for f in range(NF)], axis=0
        )
        for b in range(4)
    ]
    mine_inc = swap_blocks(per_b)

    rows_arrived(7, sq2_r, NS - 1, (after, c))
    total = jnp.sum(jnp.sum(sq2_r[:, 0, :], axis=0, keepdims=True), axis=1, keepdims=True)
    scale = step_scale / jnp.sqrt(total * (1.0 / CELLS) + epsilon)
    for i in range(4):
        out[pl.ds(i, 40, stride=4), :] = own[i] + mine_inc[i] * scale
    for copy in sent:
        copy.wait_send()


def rows_of(array):
    lead = array.shape[:-2]
    array = array.reshape(*lead, 4, 8, 128)
    return jnp.swapaxes(array, -3, -2).reshape(-1, 128)


def shards(adjoint, source, shape_grad, lower_band, upper_band, jacobian, left, right, ctrl_local):
    vmem = pltpu.VMEM
    hbm = pl.BlockSpec(memory_space=pl.ANY)
    out, sens = pl.pallas_call(
        kernel,
        out_shape=(jax.ShapeDtypeStruct((160, 128), F32), jax.ShapeDtypeStruct((8, 128), F32)),
        in_specs=[hbm] * 9,
        out_specs=(pl.BlockSpec(memory_space=vmem),) * 2,
        scratch_shapes=[
            pltpu.SMEM((NF, NF), F32),
            pltpu.SMEM((NF, NF), F32),
            pltpu.SMEM((NF, NF), F32),
            vmem((160, 128), F32),
            vmem((160, 128), F32),
            vmem((160, 128), F32),
            vmem((320, 128), F32),
            vmem((480, 128), F32),
            vmem((32, 128), jnp.int32),
            vmem((120, 128), F32),
            vmem((120, 128), F32),
            vmem((40, 128), F32),
            vmem((40, 128), F32),
            vmem((512, 128), F32),
            vmem((512, 128), F32),
            vmem((512, 128), F32),
            vmem((512, 128), F32),
            vmem((256, 128), F32),
            vmem((256, 128), F32),
            vmem((128, 4096), jnp.bfloat16),
            vmem((256, 4096), jnp.bfloat16),
            vmem((16, 8, 128), F32),
            vmem((16, 8, 128), F32),
            vmem((8, 128), F32),
            vmem((16, 8, 128), F32),
            vmem((8, 128), F32),
            vmem((32, 8, 128), F32),
            vmem((6, 40, 128), F32),
            vmem((2, 40, 128), F32),
            pltpu.SemaphoreType.DMA((9,)),
            pltpu.SemaphoreType.DMA((10,)),
            pltpu.SemaphoreType.DMA((10,)),
        ],
        compiler_params=pltpu.CompilerParams(
            collective_id=0, has_side_effects=True, vmem_limit_bytes=40 * 2**20
        ),
    )(
        *(pltpu.with_memory_space_constraint(x, pltpu.HBM) for x in (
        jacobian, left, right,
        rows_of(adjoint), rows_of(source), rows_of(shape_grad), rows_of(lower_band),
        rows_of(upper_band), rows_of(ctrl_local)))
    )
    adjoint_next = jnp.swapaxes(out.reshape(NF, 8, 4, 128), 1, 2).reshape(NF, 4, 1024)
    return adjoint_next, sens.reshape(1024)


def solution(mesh):
    cells = P(None, "stream", "cross")
    bands = P(None, None, "stream", "cross")
    in_specs = (cells, cells, cells, bands, bands, P(), P(), P(), P("stream", "cross"))
    out_specs = (cells, P(("stream", "cross")))
    return jax.shard_map(shards, mesh=mesh, in_specs=in_specs, out_specs=out_specs, check_vma=False)
```
